256 devices in a mesh: blk: 32 (over y_hi, z, core), rep: 8 (over x, y_lo).
Axes of the slice: x: 4, y: 4 (y_hi: 2, y_lo: 2; y = y_hi * 2 + y_lo), z: 8, core: 2. Of those that a mesh axis runs over, the one named last changes fastest.
Arguments:
- amplitudes: float32 [512, 512, 1024], P('blk', 'rep'), may hold values from -6 to 6
- integrals: float32 [512, 512, 4, 512], P('blk', 'rep'), may hold values from -0.01171875 to 0.01171875
- occ_energy: float32 [64], replicated, may hold values from -2 to -0.5
- virt_energy: float32 [512], replicated, may hold values from 0.3 to 3
- outer_energy: float32 [4], replicated, may hold values from 0.3 to 3
Outputs:
- update: float32 [1024, 2048], P('blk', 'rep')
The draws below stay inside these ranges and needn't reach their ends.
All inputs are finite; a program needn't handle non-finite values.
Results may differ from the reference program's by a relative error of at most 0.00028.
Values sent between devices are 32-bit elements; how exact they have to be, the bound alone decides.
A program may use at most 64 MiB of HBM per device.

```python
import jax
import jax.numpy as jnp
from jax import lax

NOCC = 64
NV = 512
A_OUT = 4
I_ROWS = 16
PAIRS = 1024


def with_spikes(entries, rng, source, target, shards_of, factor):
    def block_of(axis_at):
        return (jnp.arange(entries.shape[axis_at]) // (entries.shape[axis_at] // shards_of)).reshape((-1,) + (1,) * (entries.ndim - 1 - axis_at))

    near = jax.random.permutation(rng, shards_of)[block_of(target)]
    other_side = (block_of(target) + shards_of // 2) % shards_of
    return jnp.where((block_of(source) == near) | (block_of(source) == other_side), factor * entries, entries)


def block_levels(own_key, dims, split, smallest, largest):
    def one(axis_at, parts):
        draws = jax.random.uniform(jax.random.fold_in(jax.random.fold_in(own_key, 6), axis_at), (parts,), jnp.float32, smallest / len(split), largest / len(split))
        return jnp.repeat(jnp.exp(draws), dims[axis_at] // parts).reshape((-1,) + (1,) * (len(dims) - axis_at - 1))

    level = one(*split[0])
    for cut in split[1:]:
        level = level * one(*cut)
    return level


def scatter_about(rng, shape, spread, most, cuts=(), dtype=jnp.bfloat16):
    entries = spread * jax.random.normal(rng, shape, jnp.float32)
    if cuts:
        entries = entries * block_levels(rng, shape, cuts, -0.22, 0.18)
    return jnp.clip(entries, -most, most).astype(dtype)


def gaussian_with(key, extent, spread, most, split, heavy, kind=jnp.bfloat16):
    entries = spread * jax.random.normal(key, extent, jnp.float32)
    if split:
        entries = entries * block_levels(key, extent, split, -0.22, 0.18)
    return jnp.clip(with_spikes(entries, jax.random.fold_in(key, 3), *heavy), -most, most).astype(kind)


def setup_inputs(seed: int = 0) -> dict:
    splits = jax.random.split(jax.random.key(seed), 6)
    return {
        "amplitudes": gaussian_with(splits[0], (NV, NV, PAIRS), 1.0, 6.0, ((0, 32), (1, 8)), (0, 2, 32, 2.75), jnp.float32),
        "integrals": scatter_about(splits[1], (NV, NV, A_OUT, NV), (NV * NV) ** -0.5, 0.01171875, ((0, 32), (1, 8)), jnp.float32),
        "occ_energy": jnp.clip(jax.random.uniform(splits[2], (NOCC,), jnp.float32, -2.0, -0.5), -2.0, -0.5),
        "virt_energy": jnp.clip(jax.random.uniform(splits[3], (NV,), jnp.float32, 0.3, 3.0), 0.3, 3.0),
        "outer_energy": jnp.clip(jax.random.uniform(splits[4], (A_OUT,), jnp.float32, 0.3, 3.0), 0.3, 3.0),
    }


def reference(amplitudes, integrals, occ_energy, virt_energy, outer_energy):
    inner = NV * NV
    tmat = amplitudes.reshape(inner, PAIRS)
    wmat = integrals.reshape(inner, A_OUT * NV)
    ladder = lax.dot_general(tmat, wmat, (((0,), (0,)), ((), ())), precision=lax.Precision.HIGHEST, preferred_element_type=jnp.float32)
    pair_energy = jnp.repeat(occ_energy[:I_ROWS], NOCC) + jnp.tile(occ_energy, I_ROWS)
    column_energy = jnp.repeat(outer_energy, NV) + jnp.tile(virt_energy, A_OUT)
    return ladder / (column_energy[None, :] - pair_energy[:, None])
```

```python
import jax
import jax.numpy as jnp
from jax import lax
from jax.experimental import pallas as pl
from jax.experimental.pallas import tpu as pltpu
from jax.sharding import PartitionSpec as P

MESH = pl.DeviceIdType.MESH
F32 = jnp.float32
BF16 = jnp.bfloat16

NX, NY, NZ = 4, 4, 8
ROWS, COLS = 32, 256
UNITS = 8
LANES = 128
TOP = 24


def copy_to(src, dst, sems, at, device):
    return pltpu.make_async_remote_copy(
        src_ref=src,
        dst_ref=dst,
        send_sem=sems[0].at[at],
        recv_sem=sems[1].at[at],
        device_id=device,
        device_id_type=MESH,
    )


def kernel(
    t_hbm, w_hbm, out_ref,
    t_raw, w_raw, tcat, wcat, own, sent, got, hx, hy, hz,
    rx1, rx2, ry1, ry2, rzh, rz, rx3, rx4, ry3, ry4, rz5, rz6, rf, rz7,
    load_t, load_w,
    c_s, c_r, x1_s, x1_r, x2_s, x2_r, y1_s, y1_r, y2_s, y2_r, zh_s, zh_r, z_s, z_r,
    x3_s, x3_r, x4_s, x4_r, y3_s, y3_r, y4_s, y4_r, z5_s, z5_r, z6_s, z6_r,
    f_s, f_r, z7_s, z7_r,
):
    depth = t_hbm.shape[0]
    blk, rep = lax.axis_index("blk"), lax.axis_index("rep")
    core, z, y_hi = blk % 2, (blk // 2) % NZ, blk // (2 * NZ)
    x, y_lo = rep // 2, rep % 2
    y = 2 * y_hi + y_lo

    def along_x(d):
        return (blk, ((x + d + NX) % NX) * 2 + y_lo)

    def along_y(d):
        there = (y + d + NY) % NY
        return ((there // 2) * 2 * NZ + z * 2 + core, x * 2 + there % 2)

    def along_z(d):
        return (y_hi * 2 * NZ + ((z + d + NZ) % NZ) * 2 + core, rep)

    other_core = (blk + 1 - 2 * core, rep)
    z_at = lambda d: (z + d + NZ) % NZ
    yh_right = ((y + 1) % NY) // 2
    yh_left = ((y + 3) % NY) // 2

    barrier = pltpu.get_barrier_semaphore()
    friends = [other_core, along_x(1), along_x(-1), along_y(1), along_y(-1), along_y(2)]
    friends += [along_z(d) for d in range(1, NZ)]
    for friend in friends:
        pl.semaphore_signal(barrier, inc=1, device_id=friend, device_id_type=MESH)

    t_loads = [
        pltpu.make_async_copy(t_hbm.at[:, pl.ds(LANES * j, LANES)], t_raw.at[j], load_t.at[j])
        for j in range(8)
    ]
    part = w_hbm.shape[0] // 8
    w_loads = [
        pltpu.make_async_copy(
            w_hbm.at[pl.ds(part * j, part)], w_raw.at[pl.ds(part * j, part)], load_w.at[j]
        )
        for j in range(8)
    ]
    for load in t_loads + w_loads:
        load.start()

    step = 256

    def split(value):
        high = value.astype(BF16)
        return high, (value - high.astype(F32)).astype(BF16)

    def turn(j, _):
        pltpu.make_async_copy(t_hbm.at[:, pl.ds(0, LANES)], t_raw.at[j], load_t.at[j]).wait()
        for k in range(0, depth, step):
            high, low = split(t_raw[j, k : k + step, :].T)
            for m in range(4):
                rows = pl.ds(pl.multiple_of(64 * j + 32 * (m // 2), 32), 32)
                these = slice(32 * m, 32 * m + 32)
                tcat[m % 2, rows, k : k + step] = high[these]
                tcat[m % 2, rows, depth + k : depth + k + step] = low[these]
                tcat[m % 2, rows, 2 * depth + k : 2 * depth + k + step] = high[these]
        return 0

    lax.fori_loop(0, 8, turn, 0)
    for load in w_loads:
        load.wait()
    pl.semaphore_wait(barrier, len(friends))

    def take_columns(u):
        h, i = u // 4, u % 4
        ahead = (i // 2) * 3 * (3 - i) + (1 - i // 2) * (2 - i)
        a = (x + ahead) % NX
        b = (y_lo + h) % 2
        for c in range(2):
            for k in range(0, depth, step):
                start = k * 16 + (2 * b + c) * 4 + a
                high, low = split(w_raw[pl.ds(start, step, stride=16), :])
                lanes = slice(c * LANES, (c + 1) * LANES)
                wcat[k : k + step, lanes] = high
                wcat[depth + k : depth + k + step, lanes] = high
                wcat[2 * depth + k : 2 * depth + k + step, lanes] = low

    def product(which):
        value = jnp.dot(tcat[which], wcat[...], preferred_element_type=F32)
        return value.reshape(16, ROWS, COLS)

    def to_core(u):
        return copy_to(sent.at[u], got.at[u], (c_s, c_r), u, other_core)

    def x1(h, d):
        return copy_to(hx.at[h, 0, d], rx1.at[h, d], (x1_s, x1_r), (h, d), along_x(1 - 2 * d))

    def x2(h, d, half):
        return copy_to(
            hx.at[h, 1 + d, half], rx2.at[h, d, half], (x2_s, x2_r), (h, d, half), along_x(1 - 2 * d)
        )

    def x_final(h):
        for half in range(2):
            for d in range(2):
                x2(h, d, half).wait_recv()
            hx[h, 3, half] = hx[h, 3, half] + rx2[h, 0, half] + rx2[h, 1, half]

    def y1(i, d):
        return copy_to(
            hy.at[0, i, 1 - y_hi, pl.ds(4 * d, 4)], ry1.at[i, d], (y1_s, y1_r), (i, d), along_y(1 - 2 * d)
        )

    def y2(i, d):
        return copy_to(
            hy.at[1, i, (yh_right, yh_left)[d]], ry2.at[i, d], (y2_s, y2_r), (i, d), along_y(1 - 2 * d)
        )

    def y_next(i, d):
        yh, these = (yh_right, yh_left)[d], pl.ds(4 * d, 4)
        y1(i, d).wait_recv()
        hy[1, i, yh, these] = hy[1, i, yh, these] + ry1[i, d]
        y2(i, d).start()

    def zh(q, d):
        return copy_to(
            hz.at[q // 2, q % 2, :, d, z_at(4)], rzh.at[q, d], (zh_s, zh_r), (q, d), along_z(1 - 2 * d)
        )

    def zf(q, d, s):
        chunk = z_at((1 - 2 * d) * (3 - s))
        return copy_to(
            hz.at[q // 2, q % 2, :, :, chunk], rz.at[q, d, s], (z_s, z_r), (q, d, s), along_z(1 - 2 * d)
        )

    def z_second(q):
        for d in range(2):
            chunk = z_at((1 - 2 * d) * 3)
            zh(q, d).wait_recv()
            hz[q // 2, q % 2, :, d, chunk] = hz[q // 2, q % 2, :, d, chunk] + rzh[q, d]
            zf(q, d, 0).start()

    def z_later(q, s):
        for d in range(2):
            chunk = z_at((1 - 2 * d) * (3 - s))
            zf(q, d, s - 1).wait_recv()
            hz[q // 2, q % 2, :, :, chunk] = hz[q // 2, q % 2, :, :, chunk] + rz[q, d, s - 1]
            zf(q, d, s).start()

    def z_final(q):
        for d in range(2):
            zf(q, d, 2).wait_recv()
        h, g = q // 2, q % 2
        hz[h, g, :, :, z] = hz[h, g, :, :, z] + rz[q, 0, 2] + rz[q, 1, 2]

    def z_steps(u):
        even = u % 2 == 0

        @pl.when(jnp.logical_not(even) & (u < 8))
        def _():
            for d in range(2):
                zh(u // 2, d).start()

        @pl.when(even & (u >= 2) & (u < 10))
        def _():
            z_second(u // 2 - 1)

        @pl.when(jnp.logical_not(even) & (u >= 3) & (u < 11))
        def _():
            z_later((u - 3) // 2, 1)

        @pl.when(even & (u >= 4) & (u < 12))
        def _():
            z_later(u // 2 - 2, 2)

        @pl.when(jnp.logical_not(even) & (u >= 5))
        def _():
            z_final((u - 5) // 2)

    def x3(d):
        return copy_to(hx.at[0, 3, 1 - y_hi, pl.ds(4 * d, 4)], rx3.at[d], (x3_s, x3_r), d, along_y(1 - 2 * d))

    def x4(d):
        return copy_to(hx.at[1, 3, (yh_right, yh_left)[d]], rx4.at[d], (x4_s, x4_r), d, along_y(1 - 2 * d))

    def y3(d):
        return copy_to(hy.at[0, 0, y_hi, pl.ds(4 * d, 4)], ry3.at[d], (y3_s, y3_r), d, along_x(1 - 2 * d))

    def y4(d):
        return copy_to(hy.at[0, 1 + d, y_hi], ry4.at[d], (y4_s, y4_r), d, along_x(1 - 2 * d))

    def z5(d):
        return copy_to(hz.at[d, 0, 0, :, z], rz5.at[d], (z5_s, z5_r), d, along_x(1 - 2 * d))

    def z6(d):
        return copy_to(hz.at[:, d, 1 - d, :, z], rz6.at[d], (z6_s, z6_r), d, along_x(1 - 2 * d))

    def last(p, d):
        src = hx.at[0, 3, y_hi, z_at(d)] if p == 0 else hy.at[0, 3, y_hi, z_at(d)]
        return copy_to(src, rf.at[p, d - 1], (f_s, f_r), (p, d - 1), along_z(d))

    def z7(d):
        src = hz.at[1, 1, 1, (yh_right, yh_left)[d], z] if d < 2 else hz.at[0, 1, 1, 1 - y_hi, z]
        return copy_to(src, rz7.at[d], (z7_s, z7_r), d, along_y((1, -1, 2)[d]))

    def events(u):
        h, i = u // 4, u % 4
        to_core(u).wait_recv()
        for half in range(2):
            rows = pl.ds(8 * half, 8)
            hx[h, i, half] = own[u % 2, rows, :TOP, :LANES] + got[u, rows, :TOP, :LANES]
            hy[h, i, half] = own[u % 2, rows, :TOP, LANES:] + got[u, rows, :TOP, LANES:]
            hz[h, i // 2, i % 2, half] = own[u % 2, rows, TOP:, :] + got[u, rows, TOP:, :]

        @pl.when(i == 0)
        def _():
            for d in range(2):
                x1(h, d).start()

        @pl.when(i == 1)
        def _():
            x2(h, 0, 1).start()

        @pl.when(i == 2)
        def _():
            x2(h, 1, 0).start()
            x1(h, 0).wait_recv()
            hx[h, 1, 0] = hx[h, 1, 0] + rx1[h, 0]
            x2(h, 0, 0).start()

        @pl.when(i == 3)
        def _():
            x1(h, 1).wait_recv()
            hx[h, 2, 1] = hx[h, 2, 1] + rx1[h, 1]
            x2(h, 1, 1).start()

        @pl.when(h == 0)
        def _():
            for d in range(2):
                y1(i, d).start()

        @pl.when(h == 1)
        def _():
            for d in range(2):
                y_next(i, d)

        z_steps(u)

        @pl.when(u == 7)
        def _():
            x_final(0)
            for d in range(2):
                x3(d).start()

    def turn_units(v, _):
        @pl.when(v < UNITS)
        def _():
            take_columns(v)
            sent[v] = product(1 - core)
            to_core(v).start()

        @pl.when(v > 0)
        def _():
            events(v - 1)

        @pl.when(v < UNITS)
        def _():
            own[v % 2] = product(core)

        return 0

    lax.fori_loop(0, UNITS + 1, turn_units, 0)
    lax.fori_loop(UNITS, 12, lambda u, _: (z_steps(u), 0)[1], 0)

    for d in range(2):
        z5(d).start()
    x_final(1)
    for d in range(2):
        yh, these = (yh_right, yh_left)[d], pl.ds(4 * d, 4)
        x3(d).wait_recv()
        hx[1, 3, yh, these] = hx[1, 3, yh, these] + rx3[d]
        x4(d).start()
    for i in range(4):
        for d in range(2):
            y2(i, d).wait_recv()
        hy[0, i, y_hi] = hy[0, i, y_hi] + ry2[i, 0] + ry2[i, 1]
        if i == 0:
            for d in range(2):
                y3(d).start()
    for d in range(2):
        z5(d).wait_recv()
        hz[d, d, 1 - d, :, z] = hz[d, d, 1 - d, :, z] + rz5[d]
        z6(d).start()
    for d in range(2):
        these = pl.ds(4 * d, 4)
        y3(d).wait_recv()
        hy[0, 1 + d, y_hi, these] = hy[0, 1 + d, y_hi, these] + ry3[d]
        y4(d).start()
    for d in range(2):
        x4(d).wait_recv()
    hx[0, 3, y_hi] = hx[0, 3, y_hi] + rx4[0] + rx4[1]
    for d in range(1, NZ):
        last(0, d).start()
    for d in range(2):
        z6(d).wait_recv()
    hz[:, 1, 1, :, z] = hz[:, 1, 1, :, z] + rz6[0] + rz6[1]
    for d in range(3):
        z7(d).start()
    for d in range(2):
        y4(d).wait_recv()
    hy[0, 3, y_hi] = hy[0, 3, y_hi] + ry4[0] + ry4[1]
    for d in range(1, NZ):
        last(1, d).start()

    for p, mine in ((0, hx), (1, hy)):
        total = mine[0, 3, y_hi, z]
        for d in range(1, NZ):
            last(p, d).wait_recv()
            total = total + rf[p, d - 1]
        out_ref[:TOP, p * LANES : (p + 1) * LANES] = total
    total = hz[0, 1, 1, y_hi, z]
    for d in range(3):
        z7(d).wait_recv()
        total = total + rz7[d]
    out_ref[TOP:, :] = total

    def sent_all(u, _):
        to_core(u).wait_send()
        return 0

    def sent_groups(q, _):
        for d in range(2):
            y1(q, d).wait_send()
            y2(q, d).wait_send()
            zh(q, d).wait_send()
            for s in range(3):
                zf(q, d, s).wait_send()
        return 0

    lax.fori_loop(0, UNITS, sent_all, 0)
    lax.fori_loop(0, 4, sent_groups, 0)
    for d in range(2):
        for h in range(2):
            x1(h, d).wait_send()
            for half in range(2):
                x2(h, d, half).wait_send()
        for sending in (x3, x4, y3, y4, z5, z6):
            sending(d).wait_send()
    for d in range(1, NZ):
        for p in range(2):
            last(p, d).wait_send()
    for d in range(3):
        z7(d).wait_send()


def reduced(t, w):
    depth = t.shape[0]
    buffers = [
        ((8, depth, LANES), F32),
        (w.shape, F32),
        ((2, 16 * ROWS, 3 * depth), BF16),
        ((3 * depth, COLS), BF16),
        ((2, 16, ROWS, COLS), F32),
        ((UNITS, 16, ROWS, COLS), F32),
        ((UNITS, 16, ROWS, COLS), F32),
        ((2, 4, 2, 8, TOP, LANES), F32),
        ((2, 4, 2, 8, TOP, LANES), F32),
        ((2, 2, 2, 2, 8, ROWS - TOP, COLS), F32),
        ((2, 2, 8, TOP, LANES), F32),
        ((2, 2, 2, 8, TOP, LANES), F32),
        ((4, 2, 4, TOP, LANES), F32),
        ((4, 2, 8, TOP, LANES), F32),
        ((4, 2, 2, ROWS - TOP, COLS), F32),
        ((4, 2, 3, 2, 2, ROWS - TOP, COLS), F32),
        ((2, 4, TOP, LANES), F32),
        ((2, 8, TOP, LANES), F32),
        ((2, 4, TOP, LANES), F32),
        ((2, 8, TOP, LANES), F32),
        ((2, 2, ROWS - TOP, COLS), F32),
        ((2, 2, 2, ROWS - TOP, COLS), F32),
        ((2, 7, TOP, LANES), F32),
        ((3, ROWS - TOP, COLS), F32),
    ]
    pairs = [(8,), (2, 2), (2, 2, 2), (4, 2), (4, 2), (4, 2), (4, 2, 3)] + [(2,)] * 6 + [(2, 7), (3,)]
    sems = [pltpu.SemaphoreType.DMA((8,))] * 2
    for shape in pairs:
        sems += [pltpu.SemaphoreType.DMA(shape)] * 2
    return pl.pallas_call(
        kernel,
        out_shape=jax.ShapeDtypeStruct((ROWS, COLS), F32),
        in_specs=[pl.BlockSpec(memory_space=pl.ANY)] * 2,
        out_specs=pl.BlockSpec(memory_space=pltpu.VMEM),
        scratch_shapes=[pltpu.VMEM(shape, kind) for shape, kind in buffers] + sems,
        compiler_params=pltpu.CompilerParams(
            collective_id=0, has_side_effects=True, vmem_limit_bytes=56 * 2**20
        ),
    )(t, w)


def shards(amplitudes, integrals, occ_energy, virt_energy, outer_energy):
    depth = amplitudes.shape[0] * amplitudes.shape[1]
    t = amplitudes.reshape(depth, amplitudes.shape[2])
    w = integrals.reshape(depth, 4, 4, LANES).transpose(0, 2, 1, 3).reshape(depth * 16, LANES)
    summed = reduced(t, w)
    blk, rep = lax.axis_index("blk"), lax.axis_index("rep")
    first = lax.dynamic_slice_in_dim(occ_energy, blk // 2, 1, 0)
    second = lax.dynamic_slice_in_dim(occ_energy, (blk % 2) * ROWS, ROWS, 0)
    outer = lax.dynamic_slice_in_dim(outer_energy, rep // 2, 1, 0)
    virt = lax.dynamic_slice_in_dim(virt_energy, (rep % 2) * COLS, COLS, 0)
    return summed / ((outer + virt)[None, :] - (first + second)[:, None])


def solution(mesh):
    placed = (P("blk", "rep", None), P("blk", "rep", None, None), P(), P(), P())
    return jax.shard_map(
        shards, mesh=mesh, in_specs=placed, out_specs=P("blk", "rep"), check_vma=False
    )
```

```python
import jax
import jax.numpy as jnp
from jax import lax
from jax.experimental import pallas as pl
from jax.experimental.pallas import tpu as pltpu
from jax.sharding import PartitionSpec as P

MESH = pl.DeviceIdType.MESH
F32 = jnp.float32
BF16 = jnp.bfloat16

NX, NY, NZ = 4, 4, 8
ROWS, COLS = 32, 256
UNITS = 8
LANES = 128
TOP = 24
LOW = ROWS - TOP

BUFFERS = {
    "t_raw": ((8, 1024, LANES), F32),
    "w_raw": ((16384, LANES), F32),
    "tcat": ((2, 2, 256, 3072), BF16),
    "wcat": ((3072, 2 * COLS), BF16),
    "own": ((2, 2, 8, ROWS, COLS), F32),
    "sent": ((UNITS, 2, 8, ROWS, COLS), F32),
    "got": ((UNITS, 2, 8, ROWS, COLS), F32),
    "hx": ((2, 4, 2, 2, 4, TOP, LANES), F32),
    "hy": ((2, 4, 2, 2, 4, TOP, LANES), F32),
    "hz": ((2, 4, 2, 2, 4, LOW, COLS), F32),
    "rx1": ((2, 2, 2, 4, TOP, LANES), F32),
    "rx2": ((2, 2, 2, 2, 4, TOP, LANES), F32),
    "ry1": ((2, 3, 2, 2, TOP, LANES), F32),
    "ryd": ((2, 4, TOP, LANES), F32),
    "ry2": ((2, 4, 2, 4, TOP, LANES), F32),
    "rzh": ((4, 2, 2, LOW, COLS), F32),
    "rz3": ((4, 2, 2, 2, LOW, COLS), F32),
    "rz2": ((4, 2, 2, 2, LOW, COLS), F32),
    "rz1": ((4, 2, 2, 2, LOW, COLS), F32),
    "rx3": ((2, 2, 2, TOP, LANES), F32),
    "rx4": ((2, 2, 4, TOP, LANES), F32),
    "ry3": ((2, 2, 2, TOP, LANES), F32),
    "ry4": ((2, 2, 4, TOP, LANES), F32),
    "rz5": ((3, 2, 2, LOW, COLS), F32),
    "rf": ((2, 7, TOP, LANES), F32),
    "rz7": ((3, LOW, COLS), F32),
    "virt": ((4, LANES), F32),
    "den": ((2, ROWS, LANES), F32),
}
SENDS = {
    "c": (8,), "x1": (2, 2), "x2": (2, 2, 2), "y1": (2, 3, 2), "yd": (2,), "y2": (2, 4, 2),
    "zh": (4, 2), "z3": (4, 2), "z2": (4, 2), "z1": (4, 2), "x3": (2, 2), "x4": (2, 2),
    "y3": (2, 2), "y4": (2, 2), "z5": (3,), "f": (2, 7), "z7": (3,),
}


def kernel(t_hbm, w_hbm, occ_hbm, virt_hbm, outer_hbm, out_ref, *refs):
    names = list(BUFFERS)
    (t_raw, w_raw, tcat, wcat, own, sent, got, hx, hy, hz, rx1, rx2, ry1, ryd, ry2, rzh, rz3, rz2, rz1,
     rx3, rx4, ry3, ry4, rz5, rf, rz7, virt, den) = refs[: len(names)]
    occ, outer, load_t, load_w, load_e = refs[len(names) : len(names) + 5]
    left = refs[len(names) + 5 :]
    sems = {name: (left[2 * n], left[2 * n + 1]) for n, name in enumerate(SENDS)}

    depth = t_hbm.shape[0]
    blk, rep = lax.axis_index("blk"), lax.axis_index("rep")
    core, z, y_hi = blk % 2, (blk // 2) % NZ, blk // (2 * NZ)
    x, y_lo = rep // 2, rep % 2
    y = 2 * y_hi + y_lo
    beside = (y_lo, 1 - y_lo)
    way = (1, -1)

    def along_x(d):
        return (blk, ((x + d + NX) % NX) * 2 + y_lo)

    def along_y(d):
        there = (y + d + NY) % NY
        return ((there // 2) * 2 * NZ + z * 2 + core, x * 2 + there % 2)

    def along_z(d):
        return (y_hi * 2 * NZ + ((z + d + NZ) % NZ) * 2 + core, rep)

    other_core = (blk + 1 - 2 * core, rep)

    def put(src, dst, name, at, device):
        return pltpu.make_async_remote_copy(
            src_ref=src,
            dst_ref=dst,
            send_sem=sems[name][0].at[at],
            recv_sem=sems[name][1].at[at],
            device_id=device,
            device_id_type=MESH,
        )

    barrier = pltpu.get_barrier_semaphore()
    friends = [other_core, along_x(1), along_x(-1), along_x(2), along_y(1), along_y(-1), along_y(2)]
    friends += [along_z(d) for d in range(1, NZ)]
    for friend in friends:
        pl.semaphore_signal(barrier, inc=1, device_id=friend, device_id_type=MESH)

    small = [
        pltpu.make_async_copy(occ_hbm, occ, load_e.at[0]),
        pltpu.make_async_copy(virt_hbm, virt, load_e.at[1]),
        pltpu.make_async_copy(outer_hbm, outer, load_e.at[2]),
    ]
    for j in range(8):
        pltpu.make_async_copy(t_hbm.at[:, pl.ds(LANES * j, LANES)], t_raw.at[j], load_t.at[j]).start()
    for load in small:
        load.start()
    part = w_hbm.shape[0] // 8

    def load_columns(j):
        these = pl.ds(pl.multiple_of(part * j, part), part)
        return pltpu.make_async_copy(w_hbm.at[these], w_raw.at[these], load_w.at[j])

    step = 256

    def split(value):
        high = value.astype(BF16)
        return high, (value - high.astype(F32)).astype(BF16)

    def turn(j, _):
        pltpu.make_async_copy(t_hbm.at[:, pl.ds(0, LANES)], t_raw.at[j], load_t.at[j]).wait()
        load_columns(j).start()
        g = (j // 4 + y_hi) % 2
        for k in range(0, depth, step):
            high, low = split(t_raw[j, k : k + step, :].T)
            for m in range(4):
                slot = ((2 * j + m // 2) % NZ - z - 2 + 2 * NZ) % NZ
                rows = pl.ds(pl.multiple_of(g * 128 + (slot % 4) * 32, 32), 32)
                these = slice(32 * m, 32 * m + 32)
                tcat[m % 2, slot // 4, rows, k : k + step] = high[these]
                tcat[m % 2, slot // 4, rows, depth + k : depth + k + step] = low[these]
                tcat[m % 2, slot // 4, rows, 2 * depth + k : 2 * depth + k + step] = high[these]
        return 0

    lax.fori_loop(0, 8, turn, 0)

    for load in small:
        load.wait()
    at_row = lax.broadcasted_iota(jnp.int32, (ROWS, LANES), 0)
    pair = jnp.zeros((ROWS, LANES), F32)
    for r in range(ROWS):
        pair = jnp.where(at_row == r, occ[blk // 2] + occ[(blk % 2) * ROWS + r], pair)
    for c in range(2):
        den[c] = (outer[x] + virt[pl.ds(2 * y_lo + c, 1), :]) - pair

    for j in range(8):
        load_columns(j).wait()

    def piece(v, p):
        last = v // 3
        mid = (v + 1) // 2 - 2 * last
        one = mid - (v // 2 - last)
        return mid * (1 + p) + 3 * last, p + one * (1 - 2 * p)

    def take_columns(u):
        for p in range(2):
            i, h = piece(u % 4, p)
            ahead = (i // 2) * 3 * (3 - i) + (1 - i // 2) * (2 - i)
            a = (x + ahead) % NX
            b = (y_lo + h) % 2
            for c in range(2):
                for k in range(0, depth, step):
                    start = k * 16 + (2 * b + c) * 4 + a
                    high, low = split(w_raw[pl.ds(start, step, stride=16), :])
                    lanes = slice(p * COLS + c * LANES, p * COLS + (c + 1) * LANES)
                    wcat[k : k + step, lanes] = high
                    wcat[depth + k : depth + k + step, lanes] = high
                    wcat[2 * depth + k : 2 * depth + k + step, lanes] = low

    def product(which, half, dst, at):
        value = jnp.dot(tcat[which, half], wcat[...], preferred_element_type=F32)
        for p in range(2):
            dst[at, p] = value[:, p * COLS : (p + 1) * COLS].reshape(8, ROWS, COLS)

    def to_core(u):
        return put(sent.at[u], got.at[u], "c", u, other_core)

    def x1(s, d):
        return put(hx.at[s, 0, d], rx1.at[s, d], "x1", (s, d), along_x(way[d]))

    def x2(s, d, h):
        return put(hx.at[s, 1 + d, h], rx2.at[s, d, h], "x2", (s, d, h), along_x(way[d]))

    def x_final(s):
        for h in range(2):
            for d in range(2):
                x2(s, d, h).wait_recv()
            hx[s, 3, h] = hx[s, 3, h] + rx2[s, 0, h] + rx2[s, 1, h]

    def x3(s, d):
        return put(hx.at[s, 3, 0, 1, pl.ds(2 * d, 2)], rx3.at[s, d], "x3", (s, d), along_y(way[d]))

    def x4(s, d):
        return put(hx.at[s, 3, 1, beside[d]], rx4.at[s, d], "x4", (s, d), along_y(way[d]))

    def x_on(s):
        for d in range(2):
            these = pl.ds(2 * d, 2)
            x3(s, d).wait_recv()
            hx[s, 3, 1, beside[d], these] = hx[s, 3, 1, beside[d], these] + rx3[s, d]
            x4(s, d).start()

    def y1(s, i, d):
        return put(hy.at[s, i, 0, 1, pl.ds(2 * d, 2)], ry1.at[s, i, d], "y1", (s, i, d), along_y(way[d]))

    def yd(s):
        return put(hy.at[s, 3, 0, 1], ryd.at[s], "yd", s, along_y(2))

    def y2(s, i, d):
        return put(hy.at[s, i, 1, beside[d]], ry2.at[s, i, d], "y2", (s, i, d), along_y(way[d]))

    def y_start(s, i):
        for d in range(2):
            y1(s, i, d).start()

    def y_next(s, i):
        for d in range(2):
            these = pl.ds(2 * d, 2)
            y1(s, i, d).wait_recv()
            hy[s, i, 1, beside[d], these] = hy[s, i, 1, beside[d], these] + ry1[s, i, d]
            y2(s, i, d).start()

    def y_final(s, i):
        for d in range(2):
            y2(s, i, d).wait_recv()
        total = hy[s, i, 0, 0] + ry2[s, i, 0] + ry2[s, i, 1]
        if i == 3:
            yd(s).wait_recv()
            total = total + ryd[s]
        hy[s, i, 0, 0] = total

    def y3(s, d):
        return put(hy.at[s, 0, 0, 0, pl.ds(2 * d, 2)], ry3.at[s, d], "y3", (s, d), along_x(way[d]))

    def y4(s, d):
        return put(hy.at[s, 1 + d, 0, 0], ry4.at[s, d], "y4", (s, d), along_x(way[d]))

    def y_on(s):
        for d in range(2):
            these = pl.ds(2 * d, 2)
            y3(s, d).wait_recv()
            hy[s, 1 + d, 0, 0, these] = hy[s, 1 + d, 0, 0, these] + ry3[s, d]
            y4(s, d).start()

    def zh(v, d):
        return put(hz.at[0, v, :, d, 2], rzh.at[v, d], "zh", (v, d), along_z(way[d]))

    def z3(v, d):
        return put(hz.at[0, v, :, :, 1 + 2 * d], rz3.at[v, d], "z3", (v, d), along_z(way[d]))

    def z2(v, d):
        return put(hz.at[d, v, :, :, 0], rz2.at[v, d], "z2", (v, d), along_z(2 * way[d]))

    def z1(v, d):
        return put(hz.at[1, v, :, :, 3 - 2 * d], rz1.at[v, d], "z1", (v, d), along_z(way[d]))

    def z_second(v):
        for d in range(2):
            zh(v, d).wait_recv()
            hz[0, v, :, d, 1 + 2 * d] = hz[0, v, :, d, 1 + 2 * d] + rzh[v, d]
            z3(v, d).start()

    def z_third(v, d):
        z3(v, d).wait_recv()
        hz[d, v, :, :, 0] = hz[d, v, :, :, 0] + rz3[v, d]
        z2(v, d).start()

    def z_final(v):
        for d in range(2):
            z2(v, d).wait_recv()
            z1(v, d).wait_recv()
        hz[1, v, :, :, 2] = (
            hz[1, v, :, :, 2] + (rz2[v, 0] + rz2[v, 1]) + (rz1[v, 0] + rz1[v, 1])
        )

    def z5(n):
        src = hz.at[1, 0, :, :, 2] if n == 0 else hz.at[1, 1:3, n - 1, :, 2]
        return put(src, rz5.at[n], "z5", n, along_x((2, 1, -1)[n]))

    def z7(n):
        src = hz.at[1, 3, 1, beside[n], 2] if n < 2 else hz.at[1, 3, 0, 1, 2]
        return put(src, rz7.at[n], "z7", n, along_y((1, -1, 2)[n]))

    def last(p, d):
        s, k = ((d - 2) % NZ) // 4, (d - 2) % 4
        src = hx.at[s, 3, 0, 0, k] if p == 0 else hy.at[s, 3, 0, 0, k]
        return put(src, rf.at[p, d - 1], "f", (p, d - 1), along_z(d))

    far, near = (2, 3, 4, 5), (6, 7, 1)

    def x_last(s):
        for d in range(2):
            x4(s, d).wait_recv()
        hx[s, 3, 0, 0] = hx[s, 3, 0, 0] + rx4[s, 0] + rx4[s, 1]
        for d in (far, near)[s]:
            last(0, d).start()

    def y_last(s):
        for d in range(2):
            y4(s, d).wait_recv()
        hy[s, 3, 0, 0] = hy[s, 3, 0, 0] + ry4[s, 0] + ry4[s, 1]
        for d in (far, near)[s]:
            last(1, d).start()

    def events(u):
        s, v = u // 4, u % 4
        to_core(u).wait_recv()
        for p in range(2):
            i, h = piece(v, p)
            for g in range(2):
                rows = pl.ds(4 * g, 4)
                hx[s, i, h, g] = own[u % 2, p, rows, :TOP, :LANES] + got[u, p, rows, :TOP, :LANES]
                hy[s, i, h, g] = own[u % 2, p, rows, :TOP, LANES:] + got[u, p, rows, :TOP, LANES:]
                hz[s, v, p, g] = own[u % 2, p, rows, TOP:, :] + got[u, p, rows, TOP:, :]

        @pl.when(v == 0)
        def _():
            for d in range(2):
                x1(s, d).start()
            y_start(s, 0)

        @pl.when(v == 1)
        def _():
            x2(s, 0, 1).start()
            x2(s, 1, 0).start()
            y_start(s, 2)

        @pl.when(v == 2)
        def _():
            y_start(s, 1)

        @pl.when(v == 3)
        def _():
            yd(s).start()
            for d in range(2):
                y2(s, 3, d).start()

        @pl.when(s == 0)
        def _():
            for d in range(2):
                zh(v, d).start()

        @pl.when(s == 1)
        def _():
            for d in range(2):
                z1(v, d).start()
            z_third(v, 1)

        @pl.when(v == 2)
        def _():
            for d in range(2):
                x1(s, d).wait_recv()
                hx[s, 1 + d, d] = hx[s, 1 + d, d] + rx1[s, d]
                x2(s, d, d).start()

        @pl.when((u >= 1) & (u < 5))
        def _():
            z_second(u - 1)

        @pl.when((u >= 2) & (u < 6))
        def _():
            z_third(u - 2, 0)

        @pl.when(v == 1)
        def _():
            y_next(s, 0)

        @pl.when(v == 2)
        def _():
            y_next(s, 2)

        @pl.when(v == 3)
        def _():
            y_next(s, 1)

        @pl.when(u == 5)
        def _():
            x_final(0)
            for d in range(2):
                x3(0, d).start()
            y_final(0, 0)
            for d in range(2):
                y3(0, d).start()

        @pl.when(u == 6)
        def _():
            x_on(0)
            y_final(0, 1)
            y_final(0, 2)
            y_on(0)
            y_final(0, 3)
            z_final(0)
            z5(0).start()

        @pl.when(u == 7)
        def _():
            y_final(1, 0)
            for d in range(2):
                y3(1, d).start()
            z_final(1)

    def turn_units(u, _):
        @pl.when(u < UNITS)
        def _():
            take_columns(u)
            product(1 - core, u // 4, sent, u)

            @pl.when(u == 0)
            def _():
                pl.semaphore_wait(barrier, len(friends))

            to_core(u).start()

        @pl.when(u > 0)
        def _():
            events(u - 1)

        @pl.when(u < UNITS)
        def _():
            product(core, u // 4, own, u % 2)

        return 0

    lax.fori_loop(0, UNITS + 1, turn_units, 0)

    x_last(0)
    y_last(0)
    z_final(2)
    for n in (1, 2):
        z5(n).start()
    x_final(1)
    for d in range(2):
        x3(1, d).start()
    y_final(1, 2)
    y_final(1, 1)
    y_on(1)
    z_final(3)
    for n in range(3):
        z5(n).wait_recv()
    hz[1, 3, 0, :, 2] = hz[1, 3, 0, :, 2] + rz5[0, 0] + rz5[1, 1] + rz5[2, 0]
    hz[1, 3, 1, :, 2] = hz[1, 3, 1, :, 2] + rz5[0, 1] + rz5[1, 0] + rz5[2, 1]
    for n in range(3):
        z7(n).start()
    x_on(1)
    y_final(1, 3)
    y_last(1)
    x_last(1)

    total = hz[1, 3, 0, 0, 2]
    for n in range(3):
        z7(n).wait_recv()
        total = total + rz7[n]
    for p in range(2):
        lanes = slice(p * LANES, (p + 1) * LANES)
        out_ref[TOP:, lanes] = total[:, lanes] / den[p, TOP:]
    for p, mine in ((1, hy), (0, hx)):
        total = mine[1, 3, 0, 0, 2]
        for d in far + near:
            last(p, d).wait_recv()
            total = total + rf[p, d - 1]
        out_ref[:TOP, p * LANES : (p + 1) * LANES] = total / den[p, :TOP]

    def sent_units(u, _):
        to_core(u).wait_send()
        return 0

    def sent_quarters(v, _):
        for d in range(2):
            for sending in (zh, z3, z2, z1):
                sending(v, d).wait_send()
        return 0

    def sent_halves(s, _):
        yd(s).wait_send()
        for d in range(2):
            for sending in (x1, x3, x4, y3, y4):
                sending(s, d).wait_send()
            for h in range(2):
                x2(s, d, h).wait_send()
            for i in range(3):
                y1(s, i, d).wait_send()
            for i in range(4):
                y2(s, i, d).wait_send()
        return 0

    lax.fori_loop(0, UNITS, sent_units, 0)
    lax.fori_loop(0, 4, sent_quarters, 0)
    lax.fori_loop(0, 2, sent_halves, 0)
    for n in range(3):
        z5(n).wait_send()
        z7(n).wait_send()
    for d in range(1, NZ):
        for p in range(2):
            last(p, d).wait_send()


def shards(amplitudes, integrals, occ_energy, virt_energy, outer_energy):
    depth = amplitudes.shape[0] * amplitudes.shape[1]
    t = amplitudes.reshape(depth, amplitudes.shape[2])
    w = integrals.reshape(depth, 4, 4, LANES).transpose(0, 2, 1, 3).reshape(depth * 16, LANES)
    virt = virt_energy.reshape(4, LANES)
    scratch = [pltpu.VMEM(shape, kind) for shape, kind in BUFFERS.values()]
    scratch += [pltpu.SMEM(occ_energy.shape, F32), pltpu.SMEM(outer_energy.shape, F32)]
    scratch += [pltpu.SemaphoreType.DMA((n,)) for n in (8, 8, 3)]
    for shape in SENDS.values():
        scratch += [pltpu.SemaphoreType.DMA(shape)] * 2
    return pl.pallas_call(
        kernel,
        out_shape=jax.ShapeDtypeStruct((ROWS, COLS), F32),
        in_specs=[pl.BlockSpec(memory_space=pl.ANY)] * 5,
        out_specs=pl.BlockSpec(memory_space=pltpu.VMEM),
        scratch_shapes=scratch,
        compiler_params=pltpu.CompilerParams(
            collective_id=0, has_side_effects=True, vmem_limit_bytes=56 * 2**20
        ),
    )(t, w, occ_energy, virt, outer_energy)


def solution(mesh):
    placed = (P("blk", "rep", None), P("blk", "rep", None, None), P(), P(), P())
    return jax.shard_map(
        shards, mesh=mesh, in_specs=placed, out_specs=P("blk", "rep"), check_vma=False
    )
```

```python
import jax
import jax.numpy as jnp
from jax import lax
from jax.experimental import pallas as pl
from jax.experimental.pallas import tpu as pltpu
from jax.sharding import PartitionSpec as P

MESH = pl.DeviceIdType.MESH
F32 = jnp.float32
BF16 = jnp.bfloat16

NX, NY, NZ = 4, 4, 8
ROWS, COLS = 32, 256
UNITS = 8
LANES = 128
TOP = 24
LOW = ROWS - TOP

BUFFERS = {
    "t_raw": ((8, 1024, LANES), F32),
    "w_raw": ((16384, LANES), F32),
    "tcat": ((2, 2, 256, 3072), BF16),
    "wcat": ((4, 3072, 2 * COLS), BF16),
    "own": ((2, 2, 8, ROWS, COLS), F32),
    "sent": ((UNITS, 2, 8, ROWS, COLS), F32),
    "got": ((UNITS, 2, 8, ROWS, COLS), F32),
    "hx": ((2, 4, 2, 2, 4, TOP, LANES), F32),
    "hy": ((2, 4, 2, 2, 4, TOP, LANES), F32),
    "hz": ((2, 4, 2, 2, 4, LOW, COLS), F32),
    "rx1": ((2, 2, 2, 4, TOP, LANES), F32),
    "rx2": ((2, 2, 2, 2, 4, TOP, LANES), F32),
    "ry1": ((2, 2, 2, 2, TOP, LANES), F32),
    "ryd": ((2, 2, 4, TOP, LANES), F32),
    "ry2": ((2, 4, 2, 4, TOP, LANES), F32),
    "rzh": ((4, 2, 2, LOW, COLS), F32),
    "rz3": ((4, 2, 2, 2, LOW, COLS), F32),
    "rz2": ((4, 2, 2, 2, LOW, COLS), F32),
    "rz1": ((4, 2, 2, 2, LOW, COLS), F32),
    "rx3": ((2, 2, TOP, LANES), F32),
    "rx4": ((2, 4, TOP, LANES), F32),
    "rx5": ((4, 4, TOP, LANES), F32),
    "ry3": ((2, 2, 2, TOP, LANES), F32),
    "ry4": ((2, 2, 4, TOP, LANES), F32),
    "rz5": ((3, 2, 2, LOW, COLS), F32),
    "rf": ((2, 7, TOP, LANES), F32),
    "rz7": ((3, LOW, COLS), F32),
    "virt": ((4, LANES), F32),
    "den": ((2, ROWS, LANES), F32),
}
SENDS = {
    "c": (8,), "x1": (2, 2), "x2": (2, 2, 2), "y1": (2, 2, 2), "yd": (2, 2), "y2": (2, 4, 2),
    "zh": (4, 2), "z3": (4, 2), "z2": (4, 2), "z1": (4, 2), "x3": (2,), "x4": (2,), "x5": (4, 4),
    "y3": (2, 2), "y4": (2, 2), "z5": (3,), "f": (2, 7), "z7": (3,),
}


def kernel(t_hbm, w_hbm, occ_hbm, virt_hbm, outer_hbm, out_ref, *refs):
    names = list(BUFFERS)
    (t_raw, w_raw, tcat, wcat, own, sent, got, hx, hy, hz, rx1, rx2, ry1, ryd, ry2, rzh, rz3, rz2, rz1,
     rx3, rx4, rx5, ry3, ry4, rz5, rf, rz7, virt, den) = refs[: len(names)]
    occ, outer, load_t, load_w, load_e = refs[len(names) : len(names) + 5]
    left = refs[len(names) + 5 :]
    sems = {name: (left[2 * n], left[2 * n + 1]) for n, name in enumerate(SENDS)}

    depth = t_hbm.shape[0]
    blk, rep = lax.axis_index("blk"), lax.axis_index("rep")
    core, z, y_hi = blk % 2, (blk // 2) % NZ, blk // (2 * NZ)
    x, y_lo = rep // 2, rep % 2
    y = 2 * y_hi + y_lo
    beside = (y_lo, 1 - y_lo)
    way = (1, -1)

    def along_x(d):
        return (blk, ((x + d + NX) % NX) * 2 + y_lo)

    def along_y(d):
        there = (y + d + NY) % NY
        return ((there // 2) * 2 * NZ + z * 2 + core, x * 2 + there % 2)

    def along_yz(dy, dz):
        there = (y + dy + NY) % NY
        return (
            (there // 2) * 2 * NZ + ((z + dz + NZ) % NZ) * 2 + core,
            x * 2 + there % 2,
        )

    def along_z(d):
        return (y_hi * 2 * NZ + ((z + d + NZ) % NZ) * 2 + core, rep)

    other_core = (blk + 1 - 2 * core, rep)

    def put(src, dst, name, at, device):
        return pltpu.make_async_remote_copy(
            src_ref=src,
            dst_ref=dst,
            send_sem=sems[name][0].at[at],
            recv_sem=sems[name][1].at[at],
            device_id=device,
            device_id_type=MESH,
        )

    barrier = pltpu.get_barrier_semaphore()
    friends = [other_core, along_x(1), along_x(-1), along_x(2), along_y(1), along_y(-1), along_y(2)]
    friends += [along_z(d) for d in range(1, NZ)]
    friends += [along_yz(dy, dz) for dy in (1, -1, 2) for dz in (1, -1, 2, -2)]
    for friend in friends:
        pl.semaphore_signal(barrier, inc=1, device_id=friend, device_id_type=MESH)

    small = [
        pltpu.make_async_copy(occ_hbm, occ, load_e.at[0]),
        pltpu.make_async_copy(virt_hbm, virt, load_e.at[1]),
        pltpu.make_async_copy(outer_hbm, outer, load_e.at[2]),
    ]
    for j in range(8):
        pltpu.make_async_copy(t_hbm.at[:, pl.ds(LANES * j, LANES)], t_raw.at[j], load_t.at[j]).start()
    for load in small:
        load.start()
    part = w_hbm.shape[0] // 8

    def load_columns(j):
        these = pl.ds(pl.multiple_of(part * j, part), part)
        return pltpu.make_async_copy(w_hbm.at[these], w_raw.at[these], load_w.at[j])

    step = 256

    def split(value):
        high = value.astype(BF16)
        return high, (value - high.astype(F32)).astype(BF16)

    def turn(j, _):
        pltpu.make_async_copy(t_hbm.at[:, pl.ds(0, LANES)], t_raw.at[j], load_t.at[j]).wait()
        load_columns(j).start()
        g = (j // 4 + y_hi) % 2
        for k in range(0, depth, step):
            high, low = split(t_raw[j, k : k + step, :].T)
            for m in range(4):
                slot = ((2 * j + m // 2) % NZ - z - 2 + 2 * NZ) % NZ
                rows = pl.ds(pl.multiple_of(g * 128 + (slot % 4) * 32, 32), 32)
                these = slice(32 * m, 32 * m + 32)
                tcat[m % 2, slot // 4, rows, k : k + step] = high[these]
                tcat[m % 2, slot // 4, rows, depth + k : depth + k + step] = low[these]
                tcat[m % 2, slot // 4, rows, 2 * depth + k : 2 * depth + k + step] = high[these]
        return 0

    lax.fori_loop(0, 8, turn, 0)

    for load in small:
        load.wait()
    at_row = lax.broadcasted_iota(jnp.int32, (ROWS, LANES), 0)
    pair = jnp.zeros((ROWS, LANES), F32)
    for r in range(ROWS):
        pair = jnp.where(at_row == r, occ[blk // 2] + occ[(blk % 2) * ROWS + r], pair)
    for c in range(2):
        den[c] = (outer[x] + virt[pl.ds(2 * y_lo + c, 1), :]) - pair

    def piece(v, p):
        last = v // 3
        mid = (v + 1) // 2 - 2 * last
        one = mid - (v // 2 - last)
        return mid * (1 + p) + 3 * last, p + one * (1 - 2 * p)

    def take_part(v, k, count):
        for p in range(2):
            i, h = piece(v, p)
            ahead = (i // 2) * 3 * (3 - i) + (1 - i // 2) * (2 - i)
            a = (x + ahead) % NX
            b = (y_lo + h) % 2
            for c in range(2):
                high, low = split(w_raw[pl.ds(k * 16 + (2 * b + c) * 4 + a, count, stride=16), :])
                lanes = slice(p * COLS + c * LANES, p * COLS + (c + 1) * LANES)
                for first, value in ((0, high), (depth, high), (2 * depth, low)):
                    wcat[v, pl.ds(pl.multiple_of(first + k, 128), count), lanes] = value

    def take_first(j, _):
        load_columns(j).wait()
        take_part(0, part // 16 * j, part // 16)
        return 0

    lax.fori_loop(0, 8, take_first, 0)

    def take_columns(v):
        for k in range(0, depth, step):
            take_part(v, k, step)

    def product(which, u, dst, at):
        value = jnp.dot(tcat[which, u // 4], wcat[u % 4], preferred_element_type=F32)
        for p in range(2):
            dst[at, p] = value[:, p * COLS : (p + 1) * COLS].reshape(8, ROWS, COLS)

    def to_core(u):
        return put(sent.at[u], got.at[u], "c", u, other_core)

    def x1(s, d):
        return put(hx.at[s, 0, d], rx1.at[s, d], "x1", (s, d), along_x(way[d]))

    def x2(s, d, h):
        return put(hx.at[s, 1 + d, h], rx2.at[s, d, h], "x2", (s, d, h), along_x(way[d]))

    def x_final(s):
        for h in range(2):
            for d in range(2):
                x2(s, d, h).wait_recv()
            hx[s, 3, h] = hx[s, 3, h] + rx2[s, 0, h] + rx2[s, 1, h]

    def x3(d):
        return put(hx.at[0, 3, 0, 1, pl.ds(2 * d, 2)], rx3.at[d], "x3", d, along_y(way[d]))

    def x4(d):
        return put(hx.at[0, 3, 1, beside[d]], rx4.at[d], "x4", d, along_y(way[d]))

    def x_on():
        for d in range(2):
            these = pl.ds(2 * d, 2)
            x3(d).wait_recv()
            hx[0, 3, 1, beside[d], these] = hx[0, 3, 1, beside[d], these] + rx3[d]
            x4(d).start()

    def x5(n, k):
        h, g = ((1, beside[0]), (1, beside[1]), (0, 1), (0, 0))[n]
        to = along_yz((1, -1, 2, 0)[n], (-2, -1, 0, 1)[k])
        return put(hx.at[1, 3, h, g, k], rx5.at[n, k], "x5", (n, k), to)

    owners = [(n, k) for n in (2, 0, 1, 3) for k in (0, 1, 3, 2) if (n, k) != (3, 2)]

    def y1(s, i, d):
        n = i // 2
        return put(hy.at[s, i, 0, 1, pl.ds(2 * d, 2)], ry1.at[s, n, d], "y1", (s, n, d), along_y(way[d]))

    def yd(s, i):
        return put(hy.at[s, i, 0, 1], ryd.at[s, i // 2], "yd", (s, i // 2), along_y(2))

    def y2(s, i, d):
        return put(hy.at[s, i, 1, beside[d]], ry2.at[s, i, d], "y2", (s, i, d), along_y(way[d]))

    def y_start(s, i):
        for d in range(2):
            y1(s, i, d).start()

    def y_next(s, i):
        for d in range(2):
            these = pl.ds(2 * d, 2)
            y1(s, i, d).wait_recv()
            hy[s, i, 1, beside[d], these] = hy[s, i, 1, beside[d], these] + ry1[s, i // 2, d]
            y2(s, i, d).start()

    def y_final(s, i):
        for d in range(2):
            y2(s, i, d).wait_recv()
        total = hy[s, i, 0, 0] + ry2[s, i, 0] + ry2[s, i, 1]
        if i % 2 == 1:
            yd(s, i).wait_recv()
            total = total + ryd[s, i // 2]
        hy[s, i, 0, 0] = total

    def y3(s, d):
        return put(hy.at[s, 0, 0, 0, pl.ds(2 * d, 2)], ry3.at[s, d], "y3", (s, d), along_x(way[d]))

    def y4(s, d):
        return put(hy.at[s, 1 + d, 0, 0], ry4.at[s, d], "y4", (s, d), along_x(way[d]))

    def y_on(s):
        for d in range(2):
            these = pl.ds(2 * d, 2)
            y3(s, d).wait_recv()
            hy[s, 1 + d, 0, 0, these] = hy[s, 1 + d, 0, 0, these] + ry3[s, d]
            y4(s, d).start()

    def zh(v, d):
        return put(hz.at[0, v, :, d, 2], rzh.at[v, d], "zh", (v, d), along_z(way[d]))

    def z3(v, d):
        return put(hz.at[0, v, :, :, 1 + 2 * d], rz3.at[v, d], "z3", (v, d), along_z(way[d]))

    def z2(v, d):
        return put(hz.at[d, v, :, :, 0], rz2.at[v, d], "z2", (v, d), along_z(2 * way[d]))

    def z1(v, d):
        return put(hz.at[1, v, :, :, 3 - 2 * d], rz1.at[v, d], "z1", (v, d), along_z(way[d]))

    def z_second(v):
        for d in range(2):
            zh(v, d).wait_recv()
            hz[0, v, :, d, 1 + 2 * d] = hz[0, v, :, d, 1 + 2 * d] + rzh[v, d]
            z3(v, d).start()

    def z_third(v, d):
        z3(v, d).wait_recv()
        hz[d, v, :, :, 0] = hz[d, v, :, :, 0] + rz3[v, d]
        z2(v, d).start()

    def z_final(v):
        for d in range(2):
            z2(v, d).wait_recv()
            z1(v, d).wait_recv()
        hz[1, v, :, :, 2] = (
            hz[1, v, :, :, 2] + (rz2[v, 0] + rz2[v, 1]) + (rz1[v, 0] + rz1[v, 1])
        )

    def z5(n):
        src = hz.at[1, 0, :, :, 2] if n == 0 else hz.at[1, 1:3, n - 1, :, 2]
        return put(src, rz5.at[n], "z5", n, along_x((2, 1, -1)[n]))

    def z7(n):
        src = hz.at[1, 3, 1, beside[n], 2] if n < 2 else hz.at[1, 3, 0, 1, 2]
        return put(src, rz7.at[n], "z7", n, along_y((1, -1, 2)[n]))

    def last(p, d):
        s, k = ((d - 2) % NZ) // 4, (d - 2) % 4
        src = hx.at[s, 3, 0, 0, k] if p == 0 else hy.at[s, 3, 0, 0, k]
        return put(src, rf.at[p, d - 1], "f", (p, d - 1), along_z(d))

    far, near = (2, 3, 4, 5), (6, 7, 1)

    def x_last():
        for d in range(2):
            x4(d).wait_recv()
        hx[0, 3, 0, 0] = hx[0, 3, 0, 0] + rx4[0] + rx4[1]
        for d in far:
            last(0, d).start()

    def y_last(s):
        for d in range(2):
            y4(s, d).wait_recv()
        hy[s, 3, 0, 0] = hy[s, 3, 0, 0] + ry4[s, 0] + ry4[s, 1]
        for d in (far, near)[s]:
            last(1, d).start()

    def events(u):
        s, v = u // 4, u % 4
        to_core(u).wait_recv()
        for p in range(2):
            i, h = piece(v, p)
            for g in range(2):
                rows = pl.ds(4 * g, 4)
                hx[s, i, h, g] = own[u % 2, p, rows, :TOP, :LANES] + got[u, p, rows, :TOP, :LANES]
                hy[s, i, h, g] = own[u % 2, p, rows, :TOP, LANES:] + got[u, p, rows, :TOP, LANES:]
                hz[s, v, p, g] = own[u % 2, p, rows, TOP:, :] + got[u, p, rows, TOP:, :]

        @pl.when(v == 0)
        def _():
            for d in range(2):
                x1(s, d).start()
            y_start(s, 0)

        @pl.when(v == 1)
        def _():
            x2(s, 0, 1).start()
            x2(s, 1, 0).start()
            y_start(s, 2)
            for d in range(2):
                y2(s, 1, d).start()

        @pl.when(v == 2)
        def _():
            yd(s, 1).start()

        @pl.when(v == 3)
        def _():
            yd(s, 3).start()
            for d in range(2):
                y2(s, 3, d).start()

        @pl.when(s == 0)
        def _():
            for d in range(2):
                zh(v, d).start()

        @pl.when(s == 1)
        def _():
            for d in range(2):
                z1(v, d).start()

    def late_events(u):
        s, v = u // 4, u % 4

        @pl.when(v == 2)
        def _():
            for d in range(2):
                x1(s, d).wait_recv()
                hx[s, 1 + d, d] = hx[s, 1 + d, d] + rx1[s, d]
                x2(s, d, d).start()

        @pl.when((u >= 1) & (u < 5))
        def _():
            z_second(u - 1)

        @pl.when(s == 1)
        def _():
            z_third(v, 1)

        @pl.when((u >= 3) & (u < 7))
        def _():
            z_third(u - 3, 0)

        @pl.when(v == 1)
        def _():
            y_next(s, 0)

        @pl.when(v == 2)
        def _():
            y_next(s, 2)

        @pl.when(u == 4)
        def _():
            x_final(0)
            for d in range(2):
                x3(d).start()
            y_final(0, 0)
            for d in range(2):
                y3(0, d).start()

        @pl.when(u == 5)
        def _():
            y_final(0, 1)
            y_final(0, 2)
            y_final(0, 3)

        @pl.when(u == 6)
        def _():
            x_on()
            y_on(0)
            z_final(0)
            z5(0).start()

        @pl.when(u == 7)
        def _():
            y_final(1, 0)
            for d in range(2):
                y3(1, d).start()

    def turn_units(u, _):
        @pl.when(u < UNITS)
        def _():
            product(1 - core, u, sent, u)

            @pl.when(u == 0)
            def _():
                pl.semaphore_wait(barrier, len(friends))

            to_core(u).start()

        @pl.when(u > 0)
        def _():
            events(u - 1)

        @pl.when(u < 3)
        def _():
            take_columns(u + 1)

        @pl.when(u < UNITS)
        def _():
            product(core, u, own, u % 2)

        @pl.when(u > 0)
        def _():
            late_events(u - 1)

        return 0

    lax.fori_loop(0, UNITS + 1, turn_units, 0)

    x_final(1)
    for n, k in owners:
        x5(n, k).start()
    z_final(1)
    z_final(2)
    for n in (1, 2):
        z5(n).start()
    y_final(1, 1)
    y_final(1, 2)
    y_on(1)
    x_last()
    y_last(0)
    z_final(3)
    for n in range(3):
        z5(n).wait_recv()
    hz[1, 3, 0, :, 2] = hz[1, 3, 0, :, 2] + rz5[0, 0] + rz5[1, 1] + rz5[2, 0]
    hz[1, 3, 1, :, 2] = hz[1, 3, 1, :, 2] + rz5[0, 1] + rz5[1, 0] + rz5[2, 1]
    for n in range(3):
        z7(n).start()
    y_final(1, 3)
    y_last(1)

    total = hz[1, 3, 0, 0, 2]
    for n in range(3):
        z7(n).wait_recv()
        total = total + rz7[n]
    for p in range(2):
        lanes = slice(p * LANES, (p + 1) * LANES)
        out_ref[TOP:, lanes] = total[:, lanes] / den[p, TOP:]
    total = hx[1, 3, 0, 0, 2]
    for d in far:
        last(0, d).wait_recv()
        total = total + rf[0, d - 1]
    for n, k in owners:
        x5(n, k).wait_recv()
        total = total + rx5[n, k]
    out_ref[:TOP, :LANES] = total / den[0, :TOP]
    total = hy[1, 3, 0, 0, 2]
    for d in far + near:
        last(1, d).wait_recv()
        total = total + rf[1, d - 1]
    out_ref[:TOP, LANES:] = total / den[1, :TOP]

    def sent_units(u, _):
        to_core(u).wait_send()
        return 0

    def sent_quarters(v, _):
        for d in range(2):
            for sending in (zh, z3, z2, z1):
                sending(v, d).wait_send()
        return 0

    def sent_halves(s, _):
        yd(s, 1).wait_send()
        yd(s, 3).wait_send()
        for d in range(2):
            for sending in (x1, y3, y4):
                sending(s, d).wait_send()
            for h in range(2):
                x2(s, d, h).wait_send()
            for i in (0, 2):
                y1(s, i, d).wait_send()
            for i in range(4):
                y2(s, i, d).wait_send()
        return 0

    lax.fori_loop(0, UNITS, sent_units, 0)
    lax.fori_loop(0, 4, sent_quarters, 0)
    lax.fori_loop(0, 2, sent_halves, 0)
    for n in range(3):
        z5(n).wait_send()
        z7(n).wait_send()
    for d in range(2):
        x3(d).wait_send()
        x4(d).wait_send()
    for n, k in owners:
        x5(n, k).wait_send()
    for d in far:
        last(0, d).wait_send()
    for d in far + near:
        last(1, d).wait_send()


def shards(amplitudes, integrals, occ_energy, virt_energy, outer_energy):
    depth = amplitudes.shape[0] * amplitudes.shape[1]
    t = amplitudes.reshape(depth, amplitudes.shape[2])
    w = integrals.reshape(depth, 4, 4, LANES).transpose(0, 2, 1, 3).reshape(depth * 16, LANES)
    virt = virt_energy.reshape(4, LANES)
    scratch = [pltpu.VMEM(shape, kind) for shape, kind in BUFFERS.values()]
    scratch += [pltpu.SMEM(occ_energy.shape, F32), pltpu.SMEM(outer_energy.shape, F32)]
    scratch += [pltpu.SemaphoreType.DMA((n,)) for n in (8, 8, 3)]
    for shape in SENDS.values():
        scratch += [pltpu.SemaphoreType.DMA(shape)] * 2
    return pl.pallas_call(
        kernel,
        out_shape=jax.ShapeDtypeStruct((ROWS, COLS), F32),
        in_specs=[pl.BlockSpec(memory_space=pl.ANY)] * 5,
        out_specs=pl.BlockSpec(memory_space=pltpu.VMEM),
        scratch_shapes=scratch,
        compiler_params=pltpu.CompilerParams(
            collective_id=0, has_side_effects=True, vmem_limit_bytes=56 * 2**20
        ),
    )(t, w, occ_energy, virt, outer_energy)


def solution(mesh):
    placed = (P("blk", "rep", None), P("blk", "rep", None, None), P(), P(), P())
    return jax.shard_map(
        shards, mesh=mesh, in_specs=placed, out_specs=P("blk", "rep"), check_vma=False
    )
```

```python
import jax
import jax.numpy as jnp
from jax import lax
from jax.experimental import pallas as pl
from jax.experimental.pallas import tpu as pltpu
from jax.sharding import PartitionSpec as P

MESH = pl.DeviceIdType.MESH
F32 = jnp.float32
BF16 = jnp.bfloat16

NX, NY, NZ = 4, 4, 8
ROWS, COLS = 32, 256
UNITS = 8
LANES = 128
TOP = 24
LOW = ROWS - TOP

BUFFERS = {
    "t_raw": ((8, 1024, LANES), F32),
    "w_raw": ((16384, LANES), F32),
    "tcat": ((2, 2, 256, 2048), BF16),
    "wcat": ((4, 2048, 2 * COLS), BF16),
    "own": ((2, 2, 8, ROWS, COLS), F32),
    "sent": ((UNITS, 2, 8, ROWS, COLS), F32),
    "got": ((UNITS, 2, 8, ROWS, COLS), F32),
    "hx": ((2, 4, 2, 2, 4, TOP, LANES), F32),
    "hy": ((2, 4, 2, 2, 4, TOP, LANES), F32),
    "hz": ((2, 4, 2, 2, 4, LOW, COLS), F32),
    "rx1": ((2, 2, 2, 4, TOP, LANES), F32),
    "rx2": ((2, 2, 2, 2, 4, TOP, LANES), F32),
    "ry1": ((2, 2, 2, 2, TOP, LANES), F32),
    "ryd": ((2, 2, 4, TOP, LANES), F32),
    "ry2": ((2, 4, 2, 4, TOP, LANES), F32),
    "rzh": ((4, 2, 2, LOW, COLS), F32),
    "rz3": ((4, 2, 2, 2, LOW, COLS), F32),
    "rz2": ((4, 2, 2, 2, LOW, COLS), F32),
    "rz1": ((4, 2, 2, 2, LOW, COLS), F32),
    "rx3": ((2, 2, TOP, LANES), F32),
    "rx4": ((2, 4, TOP, LANES), F32),
    "rx5": ((4, 4, TOP, LANES), F32),
    "ry3": ((2, 2, 2, TOP, LANES), F32),
    "ry4": ((2, 2, 4, TOP, LANES), F32),
    "rz5": ((3, 2, 2, LOW, COLS), F32),
    "rf": ((2, 7, TOP, LANES), F32),
    "rz7": ((3, LOW, COLS), F32),
    "virt": ((4, LANES), F32),
    "den": ((2, ROWS, LANES), F32),
}
SENDS = {
    "c": (8,), "x1": (2, 2), "x2": (2, 2, 2), "y1": (2, 2, 2), "yd": (2, 2), "y2": (2, 4, 2),
    "zh": (4, 2), "z3": (4, 2), "z2": (4, 2), "z1": (4, 2), "x3": (2,), "x4": (2,), "x5": (4, 4),
    "y3": (2, 2), "y4": (2, 2), "z5": (3,), "f": (2, 7), "z7": (3,),
}


def kernel(t_hbm, w_hbm, occ_hbm, virt_hbm, outer_hbm, out_ref, *refs):
    names = list(BUFFERS)
    (t_raw, w_raw, tcat, wcat, own, sent, got, hx, hy, hz, rx1, rx2, ry1, ryd, ry2, rzh, rz3, rz2, rz1,
     rx3, rx4, rx5, ry3, ry4, rz5, rf, rz7, virt, den) = refs[: len(names)]
    occ, outer, load_t, load_w, load_e = refs[len(names) : len(names) + 5]
    left = refs[len(names) + 5 :]
    sems = {name: (left[2 * n], left[2 * n + 1]) for n, name in enumerate(SENDS)}

    depth = t_hbm.shape[0]
    blk, rep = lax.axis_index("blk"), lax.axis_index("rep")
    core, z, y_hi = blk % 2, (blk // 2) % NZ, blk // (2 * NZ)
    x, y_lo = rep // 2, rep % 2
    y = 2 * y_hi + y_lo
    beside = (y_lo, 1 - y_lo)
    way = (1, -1)

    def along_x(d):
        return (blk, ((x + d + NX) % NX) * 2 + y_lo)

    def along_y(d):
        there = (y + d + NY) % NY
        return ((there // 2) * 2 * NZ + z * 2 + core, x * 2 + there % 2)

    def along_yz(dy, dz):
        there = (y + dy + NY) % NY
        return (
            (there // 2) * 2 * NZ + ((z + dz + NZ) % NZ) * 2 + core,
            x * 2 + there % 2,
        )

    def along_z(d):
        return (y_hi * 2 * NZ + ((z + d + NZ) % NZ) * 2 + core, rep)

    other_core = (blk + 1 - 2 * core, rep)
    at_x = {d: along_x(d) for d in (1, -1, 2)}
    at_y = {d: along_y(d) for d in (1, -1, 2)}
    at_z = {d: along_z(d) for d in (1, -1, 2, -2, 3, 4, 5, 6, 7)}
    at_yz = {(dy, dz): along_yz(dy, dz) for dy in (1, -1, 2) for dz in (1, -1, 2, -2)}
    at_yz.update({(dy, 0): at_y[dy] for dy in at_y})
    at_yz.update({(0, dz): at_z[dz] for dz in (1, -1, -2)})

    def put(src, dst, name, at, device):
        return pltpu.make_async_remote_copy(
            src_ref=src,
            dst_ref=dst,
            send_sem=sems[name][0].at[at],
            recv_sem=sems[name][1].at[at],
            device_id=device,
            device_id_type=MESH,
        )

    barrier = pltpu.get_barrier_semaphore()
    friends = [other_core, at_x[1], at_x[-1], at_x[2], at_y[1], at_y[-1], at_y[2]]
    friends += [at_z[d] for d in range(1, NZ)]
    friends += [at_yz[dy, dz] for dy in (1, -1, 2) for dz in (1, -1, 2, -2)]
    for friend in friends:
        pl.semaphore_signal(barrier, inc=1, device_id=friend, device_id_type=MESH)

    small = [
        pltpu.make_async_copy(occ_hbm, occ, load_e.at[0]),
        pltpu.make_async_copy(virt_hbm, virt, load_e.at[1]),
        pltpu.make_async_copy(outer_hbm, outer, load_e.at[2]),
    ]
    for j in range(8):
        pltpu.make_async_copy(t_hbm.at[:, pl.ds(LANES * j, LANES)], t_raw.at[j], load_t.at[j]).start()
    for load in small:
        load.start()
    part = w_hbm.shape[0] // 8

    def load_columns(j):
        these = pl.ds(pl.multiple_of(part * j, part), part)
        return pltpu.make_async_copy(w_hbm.at[these], w_raw.at[these], load_w.at[j])

    step = 256

    def split(value):
        high = value.astype(BF16)
        return high, (value - high.astype(F32)).astype(BF16)

    def turn(j, _):
        pltpu.make_async_copy(t_hbm.at[:, pl.ds(0, LANES)], t_raw.at[j], load_t.at[j]).wait()
        load_columns(j).start()
        g = (j // 4 + y_hi) % 2
        for k in range(0, depth, step):
            high, low = split(t_raw[j, k : k + step, :].T)
            for m in range(4):
                slot = ((2 * j + m // 2) % NZ - z - 2 + 2 * NZ) % NZ
                rows = pl.ds(pl.multiple_of(g * 128 + (slot % 4) * 32, 32), 32)
                these = slice(32 * m, 32 * m + 32)
                tcat[m % 2, slot // 4, rows, k : k + step] = high[these]
                tcat[m % 2, slot // 4, rows, depth + k : depth + k + step] = low[these]
        return 0

    lax.fori_loop(0, 8, turn, 0)

    for load in small:
        load.wait()
    at_row = lax.broadcasted_iota(jnp.int32, (ROWS, LANES), 0)
    pair = jnp.zeros((ROWS, LANES), F32)
    for r in range(ROWS):
        pair = jnp.where(at_row == r, occ[blk // 2] + occ[(blk % 2) * ROWS + r], pair)
    for c in range(2):
        den[c] = (outer[x] + virt[pl.ds(2 * y_lo + c, 1), :]) - pair

    def piece(v, p):
        div = (lambda a, b: a // b) if isinstance(v, int) else lax.div
        last = div(v, 3)
        mid = div(v + 1, 2) - 2 * last
        one = mid - (div(v, 2) - last)
        return mid * (1 + p) + 3 * last, p + one * (1 - 2 * p)

    def take_part(v, k, count):
        for p in range(2):
            i, h = piece(v, p)
            ahead = (i // 2) * 3 * (3 - i) + (1 - i // 2) * (2 - i)
            a = (x + ahead) % NX
            b = (y_lo + h) % 2
            for c in range(2):
                high, low = split(w_raw[pl.ds(k * 16 + (2 * b + c) * 4 + a, count, stride=16), :])
                lanes = slice(p * COLS + c * LANES, p * COLS + (c + 1) * LANES)
                for first, value in ((0, high), (depth, low)):
                    wcat[v, pl.ds(pl.multiple_of(first + k, 128), count), lanes] = value

    def take_rows(j, _):
        load_columns(j).wait()
        for v in range(4):
            take_part(v, part // 16 * j, part // 16)
        return 0

    lax.fori_loop(0, 8, take_rows, 0)

    def product(which, u, dst, at):
        s, v = lax.div(u, 4), lax.rem(u, 4)

        def dot(a, b):
            return jnp.dot(
                tcat[which, s, :, a : a + depth], wcat[v, b : b + depth], preferred_element_type=F32
            )

        value = dot(0, 0) + dot(depth, 0) + dot(0, depth)
        for p in range(2):
            dst[at, p] = value[:, p * COLS : (p + 1) * COLS].reshape(8, ROWS, COLS)

    def to_core(u):
        return put(sent.at[u], got.at[u], "c", u, other_core)

    def x1(s, d):
        return put(hx.at[s, 0, d], rx1.at[s, d], "x1", (s, d), at_x[way[d]])

    def x2(s, d, h):
        return put(hx.at[s, 1 + d, h], rx2.at[s, d, h], "x2", (s, d, h), at_x[way[d]])

    def x_on_way(s):
        for d in range(2):
            x1(s, d).wait_recv()
            hx[s, 1 + d, d] = hx[s, 1 + d, d] + rx1[s, d]
            x2(s, d, d).start()

    def x_final(s):
        for h in range(2):
            for d in range(2):
                x2(s, d, h).wait_recv()
            hx[s, 3, h] = hx[s, 3, h] + rx2[s, 0, h] + rx2[s, 1, h]

    def x3(d):
        return put(hx.at[0, 3, 0, 1, pl.ds(2 * d, 2)], rx3.at[d], "x3", d, at_y[way[d]])

    def x4(d):
        return put(hx.at[0, 3, 1, beside[d]], rx4.at[d], "x4", d, at_y[way[d]])

    def x_on():
        for d in range(2):
            these = pl.ds(2 * d, 2)
            x3(d).wait_recv()
            hx[0, 3, 1, beside[d], these] = hx[0, 3, 1, beside[d], these] + rx3[d]
            x4(d).start()

    def x5(n, k):
        h, g = ((1, beside[0]), (1, beside[1]), (0, 1), (0, 0))[n]
        to = at_yz[(1, -1, 2, 0)[n], (-2, -1, 0, 1)[k]]
        return put(hx.at[1, 3, h, g, k], rx5.at[n, k], "x5", (n, k), to)

    owners = [(n, k) for n in (2, 0, 1, 3) for k in (0, 1, 3, 2) if (n, k) != (3, 2)]

    def y1(s, i, d):
        n = i // 2
        return put(hy.at[s, i, 0, 1, pl.ds(2 * d, 2)], ry1.at[s, n, d], "y1", (s, n, d), at_y[way[d]])

    def yd(s, i):
        return put(hy.at[s, i, 0, 1], ryd.at[s, i // 2], "yd", (s, i // 2), at_y[2])

    def y2(s, i, d):
        return put(hy.at[s, i, 1, beside[d]], ry2.at[s, i, d], "y2", (s, i, d), at_y[way[d]])

    def y_start(s, i):
        for d in range(2):
            y1(s, i, d).start()

    def y_next(s, i):
        for d in range(2):
            these = pl.ds(2 * d, 2)
            y1(s, i, d).wait_recv()
            hy[s, i, 1, beside[d], these] = hy[s, i, 1, beside[d], these] + ry1[s, i // 2, d]
            y2(s, i, d).start()

    def y_final(s, i):
        for d in range(2):
            y2(s, i, d).wait_recv()
        total = hy[s, i, 0, 0] + ry2[s, i, 0] + ry2[s, i, 1]
        if i % 2 == 1:
            yd(s, i).wait_recv()
            total = total + ryd[s, i // 2]
        hy[s, i, 0, 0] = total

    def y3(s, d):
        return put(hy.at[s, 0, 0, 0, pl.ds(2 * d, 2)], ry3.at[s, d], "y3", (s, d), at_x[way[d]])

    def y4(s, d):
        return put(hy.at[s, 1 + d, 0, 0], ry4.at[s, d], "y4", (s, d), at_x[way[d]])

    def y_on(s):
        for d in range(2):
            these = pl.ds(2 * d, 2)
            y3(s, d).wait_recv()
            hy[s, 1 + d, 0, 0, these] = hy[s, 1 + d, 0, 0, these] + ry3[s, d]
            y4(s, d).start()

    def zh(v, d):
        return put(hz.at[0, v, :, d, 2], rzh.at[v, d], "zh", (v, d), at_z[way[d]])

    def z3(v, d):
        return put(hz.at[0, v, :, :, 1 + 2 * d], rz3.at[v, d], "z3", (v, d), at_z[way[d]])

    def z2(v, d):
        return put(hz.at[d, v, :, :, 0], rz2.at[v, d], "z2", (v, d), at_z[2 * way[d]])

    def z1(v, d):
        return put(hz.at[1, v, :, :, 3 - 2 * d], rz1.at[v, d], "z1", (v, d), at_z[way[d]])

    def z_second(v):
        for d in range(2):
            zh(v, d).wait_recv()
            hz[0, v, :, d, 1 + 2 * d] = hz[0, v, :, d, 1 + 2 * d] + rzh[v, d]
            z3(v, d).start()

    def z_third(v, d):
        z3(v, d).wait_recv()
        hz[d, v, :, :, 0] = hz[d, v, :, :, 0] + rz3[v, d]
        z2(v, d).start()

    def z_final(v):
        for d in range(2):
            z2(v, d).wait_recv()
            z1(v, d).wait_recv()
        hz[1, v, :, :, 2] = (
            hz[1, v, :, :, 2] + (rz2[v, 0] + rz2[v, 1]) + (rz1[v, 0] + rz1[v, 1])
        )

    def z5(n):
        src = hz.at[1, 0, :, :, 2] if n == 0 else hz.at[1, 1:3, n - 1, :, 2]
        return put(src, rz5.at[n], "z5", n, at_x[(2, 1, -1)[n]])

    def z7(n):
        src = hz.at[1, 3, 1, beside[n], 2] if n < 2 else hz.at[1, 3, 0, 1, 2]
        return put(src, rz7.at[n], "z7", n, at_y[(1, -1, 2)[n]])

    def last(p, d):
        s, k = ((d - 2) % NZ) // 4, (d - 2) % 4
        src = hx.at[s, 3, 0, 0, k] if p == 0 else hy.at[s, 3, 0, 0, k]
        return put(src, rf.at[p, d - 1], "f", (p, d - 1), at_z[d])

    far, near = (2, 3, 4, 5), (6, 7, 1)

    def x_last():
        for d in range(2):
            x4(d).wait_recv()
        hx[0, 3, 0, 0] = hx[0, 3, 0, 0] + rx4[0] + rx4[1]
        for d in far:
            last(0, d).start()

    def y_last(s):
        for d in range(2):
            y4(s, d).wait_recv()
        hy[s, 3, 0, 0] = hy[s, 3, 0, 0] + ry4[s, 0] + ry4[s, 1]
        for d in (far, near)[s]:
            last(1, d).start()

    def events(u):
        s, v = lax.div(u, 4), lax.rem(u, 4)
        to_core(u).wait_recv()
        for p in range(2):
            i, h = piece(v, p)
            for g in range(2):
                rows = pl.ds(4 * g, 4)
                hx[s, i, h, g] = own[lax.rem(u, 2), p, rows, :TOP, :LANES] + got[u, p, rows, :TOP, :LANES]
                hy[s, i, h, g] = own[lax.rem(u, 2), p, rows, :TOP, LANES:] + got[u, p, rows, :TOP, LANES:]
                hz[s, v, p, g] = own[lax.rem(u, 2), p, rows, TOP:, :] + got[u, p, rows, TOP:, :]

        @pl.when(v == 0)
        def _():
            for d in range(2):
                x1(s, d).start()
            y_start(s, 0)

        @pl.when(v == 1)
        def _():
            x2(s, 0, 1).start()
            x2(s, 1, 0).start()
            y_start(s, 2)
            for d in range(2):
                y2(s, 1, d).start()

        @pl.when(v == 2)
        def _():
            yd(s, 1).start()

        @pl.when(v == 3)
        def _():
            yd(s, 3).start()
            for d in range(2):
                y2(s, 3, d).start()

        @pl.when(s == 0)
        def _():
            for d in range(2):
                zh(v, d).start()

        @pl.when(s == 1)
        def _():
            z_third(v, 1)
            for d in range(2):
                z1(v, d).start()

        @pl.when(u == 6)
        def _():
            x_on_way(1)
            y_next(1, 2)

    def late_events(u):
        s, v = lax.div(u, 4), lax.rem(u, 4)

        @pl.when(u == 2)
        def _():
            x_on_way(0)

        @pl.when((u >= 1) & (u < 5))
        def _():
            z_second(u - 1)

        @pl.when((u >= 3) & (u < 7))
        def _():
            z_third(u - 3, 0)

        @pl.when(v == 1)
        def _():
            y_next(s, 0)

        @pl.when(u == 2)
        def _():
            y_next(0, 2)

        @pl.when(u == 4)
        def _():
            x_final(0)
            for d in range(2):
                x3(d).start()
            y_final(0, 0)
            for d in range(2):
                y3(0, d).start()

        @pl.when(u == 5)
        def _():
            y_final(0, 1)
            y_final(0, 2)
            y_final(0, 3)

        @pl.when(u == 6)
        def _():
            x_on()
            y_on(0)
            z_final(0)
            z5(0).start()

        @pl.when(u == 7)
        def _():
            y_final(1, 0)
            for d in range(2):
                y3(1, d).start()

    def turn_units(u, _):
        @pl.when(u < UNITS)
        def _():
            product(1 - core, u, sent, u)

            @pl.when(u == 0)
            def _():
                pl.semaphore_wait(barrier, len(friends))

            to_core(u).start()

        @pl.when(u > 0)
        def _():
            events(u - 1)

        @pl.when(u < UNITS)
        def _():
            product(core, u, own, lax.rem(u, 2))

        @pl.when(u > 0)
        def _():
            late_events(u - 1)

        return 0

    lax.fori_loop(0, UNITS + 1, turn_units, 0)

    x_final(1)
    for n, k in owners:
        x5(n, k).start()
    z_final(1)
    z_final(2)
    for n in (1, 2):
        z5(n).start()
    y_final(1, 1)
    y_final(1, 2)
    y_on(1)
    x_last()
    y_last(0)
    z_final(3)
    for n in range(3):
        z5(n).wait_recv()
    hz[1, 3, 0, :, 2] = hz[1, 3, 0, :, 2] + rz5[0, 0] + rz5[1, 1] + rz5[2, 0]
    hz[1, 3, 1, :, 2] = hz[1, 3, 1, :, 2] + rz5[0, 1] + rz5[1, 0] + rz5[2, 1]
    for n in range(3):
        z7(n).start()
    y_final(1, 3)
    y_last(1)

    total = hz[1, 3, 0, 0, 2]
    for n in range(3):
        z7(n).wait_recv()
        total = total + rz7[n]
    for p in range(2):
        lanes = slice(p * LANES, (p + 1) * LANES)
        out_ref[TOP:, lanes] = total[:, lanes] / den[p, TOP:]
    total = hx[1, 3, 0, 0, 2]
    for d in far:
        last(0, d).wait_recv()
        total = total + rf[0, d - 1]
    for n, k in owners:
        x5(n, k).wait_recv()
        total = total + rx5[n, k]
    out_ref[:TOP, :LANES] = total / den[0, :TOP]
    total = hy[1, 3, 0, 0, 2]
    for d in far + near:
        last(1, d).wait_recv()
        total = total + rf[1, d - 1]
    out_ref[:TOP, LANES:] = total / den[1, :TOP]

    def sent_units(u, _):
        to_core(u).wait_send()
        return 0

    def sent_quarters(v, _):
        for d in range(2):
            for sending in (zh, z3, z2, z1):
                sending(v, d).wait_send()
        return 0

    def sent_halves(s, _):
        yd(s, 1).wait_send()
        yd(s, 3).wait_send()
        for d in range(2):
            for sending in (x1, y3, y4):
                sending(s, d).wait_send()
            for h in range(2):
                x2(s, d, h).wait_send()
            for i in (0, 2):
                y1(s, i, d).wait_send()
            for i in range(4):
                y2(s, i, d).wait_send()
        return 0

    lax.fori_loop(0, UNITS, sent_units, 0)
    lax.fori_loop(0, 4, sent_quarters, 0)
    lax.fori_loop(0, 2, sent_halves, 0)
    for n in range(3):
        z5(n).wait_send()
        z7(n).wait_send()
    for d in range(2):
        x3(d).wait_send()
        x4(d).wait_send()
    for n, k in owners:
        x5(n, k).wait_send()
    for d in far:
        last(0, d).wait_send()
    for d in far + near:
        last(1, d).wait_send()


def shards(amplitudes, integrals, occ_energy, virt_energy, outer_energy):
    depth = amplitudes.shape[0] * amplitudes.shape[1]
    t = amplitudes.reshape(depth, amplitudes.shape[2])
    w = integrals.reshape(depth, 4, 4, LANES).transpose(0, 2, 1, 3).reshape(depth * 16, LANES)
    virt = virt_energy.reshape(4, LANES)
    scratch = [pltpu.VMEM(shape, kind) for shape, kind in BUFFERS.values()]
    scratch += [pltpu.SMEM(occ_energy.shape, F32), pltpu.SMEM(outer_energy.shape, F32)]
    scratch += [pltpu.SemaphoreType.DMA((n,)) for n in (8, 8, 3)]
    for shape in SENDS.values():
        scratch += [pltpu.SemaphoreType.DMA(shape)] * 2
    return pl.pallas_call(
        kernel,
        out_shape=jax.ShapeDtypeStruct((ROWS, COLS), F32),
        in_specs=[pl.BlockSpec(memory_space=pl.ANY)] * 5,
        out_specs=pl.BlockSpec(memory_space=pltpu.VMEM),
        scratch_shapes=scratch,
        compiler_params=pltpu.CompilerParams(
            collective_id=0, has_side_effects=True, vmem_limit_bytes=56 * 2**20
        ),
    )(t, w, occ_energy, virt, outer_energy)


def solution(mesh):
    placed = (P("blk", "rep", None), P("blk", "rep", None, None), P(), P(), P())
    return jax.shard_map(
        shards, mesh=mesh, in_specs=placed, out_specs=P("blk", "rep"), check_vma=False
    )
```

```python
import jax
import jax.numpy as jnp
from jax import lax
from jax.experimental import pallas as pl
from jax.experimental.pallas import tpu as pltpu
from jax.sharding import PartitionSpec as P

MESH = pl.DeviceIdType.MESH
F32 = jnp.float32
BF16 = jnp.bfloat16

NX, NY, NZ = 4, 4, 8
ROWS, COLS = 32, 256
UNITS = 8
LANES = 128
TOP = 24
LOW = ROWS - TOP

BUFFERS = {
    "t_raw": ((8, 1024, LANES), F32),
    "w_raw": ((16384, LANES), F32),
    "tcat": ((2, 2, 256, 2048), BF16),
    "wcat": ((4, 2048, 2 * COLS), BF16),
    "own": ((2, 2, 8, ROWS, COLS), F32),
    "sent": ((UNITS, 2, 8, ROWS, COLS), F32),
    "got": ((UNITS, 2, 8, ROWS, COLS), F32),
    "hx": ((2, 4, 2, 2, 4, TOP, LANES), F32),
    "hy": ((2, 4, 2, 2, 4, TOP, LANES), F32),
    "hz": ((2, 4, 2, 2, 4, LOW, COLS), F32),
    "rx1": ((2, 2, 2, 4, TOP, LANES), F32),
    "rx2": ((2, 2, 2, 2, 4, TOP, LANES), F32),
    "ry1": ((2, 2, 2, 2, TOP, LANES), F32),
    "ryd": ((2, 2, 4, TOP, LANES), F32),
    "ry2": ((2, 4, 2, 4, TOP, LANES), F32),
    "rzh": ((4, 2, 2, LOW, COLS), F32),
    "rz3": ((4, 2, 2, 2, LOW, COLS), F32),
    "rz2": ((4, 2, 2, 2, LOW, COLS), F32),
    "rz1": ((4, 2, 2, 2, LOW, COLS), F32),
    "rx3": ((2, 2, TOP, LANES), F32),
    "rx4": ((2, 4, TOP, LANES), F32),
    "rx5": ((4, 4, TOP, LANES), F32),
    "ry3": ((2, 2, 2, TOP, LANES), F32),
    "ry4": ((2, 2, 4, TOP, LANES), F32),
    "rz5": ((3, 2, 2, LOW, COLS), F32),
    "rf": ((2, 7, TOP, LANES), F32),
    "rz7": ((3, LOW, COLS), F32),
    "virt": ((4, LANES), F32),
    "den": ((2, ROWS, LANES), F32),
}
SENDS = {
    "c": (8,), "x1": (2, 2), "x2": (2, 2, 2), "y1": (2, 2, 2), "yd": (2, 2), "y2": (2, 4, 2),
    "zh": (4, 2), "z3": (4, 2), "z2": (4, 2), "z1": (4, 2), "x3": (2,), "x4": (2,), "x5": (4, 4),
    "y3": (2, 2), "y4": (2, 2), "z5": (3,), "f": (2, 7), "z7": (3,),
}


def kernel(t_hbm, w_hbm, occ_hbm, virt_hbm, outer_hbm, out_ref, *refs):
    names = list(BUFFERS)
    (t_raw, w_raw, tcat, wcat, own, sent, got, hx, hy, hz, rx1, rx2, ry1, ryd, ry2, rzh, rz3, rz2, rz1,
     rx3, rx4, rx5, ry3, ry4, rz5, rf, rz7, virt, den) = refs[: len(names)]
    occ, outer, load_t, load_w, load_e = refs[len(names) : len(names) + 5]
    left = refs[len(names) + 5 :]
    sems = {name: (left[2 * n], left[2 * n + 1]) for n, name in enumerate(SENDS)}

    depth = t_hbm.shape[0]
    blk, rep = lax.axis_index("blk"), lax.axis_index("rep")
    core, z, y_hi = blk % 2, (blk // 2) % NZ, blk // (2 * NZ)
    x, y_lo = rep // 2, rep % 2
    y = 2 * y_hi + y_lo
    beside = (y_lo, 1 - y_lo)
    way = (1, -1)

    def along_x(d):
        return (blk, ((x + d + NX) % NX) * 2 + y_lo)

    def along_y(d):
        there = (y + d + NY) % NY
        return ((there // 2) * 2 * NZ + z * 2 + core, x * 2 + there % 2)

    def along_yz(dy, dz):
        there = (y + dy + NY) % NY
        return (
            (there // 2) * 2 * NZ + ((z + dz + NZ) % NZ) * 2 + core,
            x * 2 + there % 2,
        )

    def along_z(d):
        return (y_hi * 2 * NZ + ((z + d + NZ) % NZ) * 2 + core, rep)

    other_core = (blk + 1 - 2 * core, rep)
    at_x = {d: along_x(d) for d in (1, -1, 2)}
    at_y = {d: along_y(d) for d in (1, -1, 2)}
    at_z = {d: along_z(d) for d in (1, -1, 2, -2, 3, 4, 5, 6, 7)}
    at_yz = {(dy, dz): along_yz(dy, dz) for dy in (1, -1, 2) for dz in (1, -1, 2, -2)}
    at_yz.update({(dy, 0): at_y[dy] for dy in at_y})
    at_yz.update({(0, dz): at_z[dz] for dz in (1, -1, -2)})

    def put(src, dst, name, at, device):
        return pltpu.make_async_remote_copy(
            src_ref=src,
            dst_ref=dst,
            send_sem=sems[name][0].at[at],
            recv_sem=sems[name][1].at[at],
            device_id=device,
            device_id_type=MESH,
        )

    barrier = pltpu.get_barrier_semaphore()
    friends = [other_core, at_x[1], at_x[-1], at_x[2], at_y[1], at_y[-1], at_y[2]]
    friends += [at_z[d] for d in range(1, NZ)]
    friends += [at_yz[dy, dz] for dy in (1, -1, 2) for dz in (1, -1, 2, -2)]
    for friend in friends:
        pl.semaphore_signal(barrier, inc=1, device_id=friend, device_id_type=MESH)

    small = [
        pltpu.make_async_copy(occ_hbm, occ, load_e.at[0]),
        pltpu.make_async_copy(virt_hbm, virt, load_e.at[1]),
        pltpu.make_async_copy(outer_hbm, outer, load_e.at[2]),
    ]
    for j in range(8):
        pltpu.make_async_copy(t_hbm.at[:, pl.ds(LANES * j, LANES)], t_raw.at[j], load_t.at[j]).start()
    for load in small:
        load.start()
    part = w_hbm.shape[0] // 8

    def load_columns(j):
        these = pl.ds(pl.multiple_of(part * j, part), part)
        return pltpu.make_async_copy(w_hbm.at[these], w_raw.at[these], load_w.at[j])

    step = 256

    def split(value):
        high = value.astype(BF16)
        return high, (value - high.astype(F32)).astype(BF16)

    def turn(j, _):
        pltpu.make_async_copy(t_hbm.at[:, pl.ds(0, LANES)], t_raw.at[j], load_t.at[j]).wait()
        load_columns(j).start()
        g = (j // 4 + y_hi) % 2
        for k in range(0, depth, step):
            high, low = split(t_raw[j, k : k + step, :].T)
            for m in range(4):
                slot = ((2 * j + m // 2) % NZ - z - 2 + 2 * NZ) % NZ
                rows = pl.ds(pl.multiple_of(g * 128 + (slot % 4) * 32, 32), 32)
                these = slice(32 * m, 32 * m + 32)
                tcat[m % 2, slot // 4, rows, k : k + step] = high[these]
                tcat[m % 2, slot // 4, rows, depth + k : depth + k + step] = low[these]
        return 0

    lax.fori_loop(0, 8, turn, 0)

    def piece(v, p):
        div = (lambda a, b: a // b) if isinstance(v, int) else lax.div
        last = div(v, 3)
        mid = div(v + 1, 2) - 2 * last
        one = mid - (div(v, 2) - last)
        return mid * (1 + p) + 3 * last, p + one * (1 - 2 * p)

    def take_part(v, k, count):
        for p in range(2):
            i, h = piece(v, p)
            ahead = (i // 2) * 3 * (3 - i) + (1 - i // 2) * (2 - i)
            a = (x + ahead) % NX
            b = (y_lo + h) % 2
            for c in range(2):
                high, low = split(w_raw[pl.ds(k * 16 + (2 * b + c) * 4 + a, count, stride=16), :])
                lanes = slice(p * COLS + c * LANES, p * COLS + (c + 1) * LANES)
                for first, value in ((0, high), (depth, low)):
                    wcat[v, pl.ds(pl.multiple_of(first + k, 128), count), lanes] = value

    def take_rows(j, _):
        load_columns(j).wait()
        for v in range(4):
            take_part(v, part // 16 * j, part // 16)
        return 0

    lax.fori_loop(0, 8, take_rows, 0)

    def product(which, u, dst, at):
        s, v = lax.div(u, 4), lax.rem(u, 4)

        def dot(a, b):
            return jnp.dot(
                tcat[which, s, :, a : a + depth], wcat[v, b : b + depth], preferred_element_type=F32
            )

        value = dot(0, 0) + dot(depth, 0) + dot(0, depth)
        for p in range(2):
            dst[at, p] = value[:, p * COLS : (p + 1) * COLS].reshape(8, ROWS, COLS)

    def to_core(u):
        return put(sent.at[u], got.at[u], "c", u, other_core)

    def x1(s, d):
        return put(hx.at[s, 0, d], rx1.at[s, d], "x1", (s, d), at_x[way[d]])

    def x2(s, d, h):
        return put(hx.at[s, 1 + d, h], rx2.at[s, d, h], "x2", (s, d, h), at_x[way[d]])

    def x_on_way(s):
        for d in range(2):
            x1(s, d).wait_recv()
            hx[s, 1 + d, d] = hx[s, 1 + d, d] + rx1[s, d]
            x2(s, d, d).start()

    def x_final(s):
        for h in range(2):
            for d in range(2):
                x2(s, d, h).wait_recv()
            hx[s, 3, h] = hx[s, 3, h] + rx2[s, 0, h] + rx2[s, 1, h]

    def x3(d):
        return put(hx.at[0, 3, 0, 1, pl.ds(2 * d, 2)], rx3.at[d], "x3", d, at_y[way[d]])

    def x4(d):
        return put(hx.at[0, 3, 1, beside[d]], rx4.at[d], "x4", d, at_y[way[d]])

    def x_on():
        for d in range(2):
            these = pl.ds(2 * d, 2)
            x3(d).wait_recv()
            hx[0, 3, 1, beside[d], these] = hx[0, 3, 1, beside[d], these] + rx3[d]
            x4(d).start()

    def x5(n, k):
        h, g = ((1, beside[0]), (1, beside[1]), (0, 1), (0, 0))[n]
        to = at_yz[(1, -1, 2, 0)[n], (-2, -1, 0, 1)[k]]
        return put(hx.at[1, 3, h, g, k], rx5.at[n, k], "x5", (n, k), to)

    owners = [(n, k) for n in (2, 0, 1, 3) for k in (0, 1, 3, 2) if (n, k) != (3, 2)]

    def y1(s, i, d):
        n = i // 2
        return put(hy.at[s, i, 0, 1, pl.ds(2 * d, 2)], ry1.at[s, n, d], "y1", (s, n, d), at_y[way[d]])

    def yd(s, i):
        return put(hy.at[s, i, 0, 1], ryd.at[s, i // 2], "yd", (s, i // 2), at_y[2])

    def y2(s, i, d):
        return put(hy.at[s, i, 1, beside[d]], ry2.at[s, i, d], "y2", (s, i, d), at_y[way[d]])

    def y_start(s, i):
        for d in range(2):
            y1(s, i, d).start()

    def y_next(s, i):
        for d in range(2):
            these = pl.ds(2 * d, 2)
            y1(s, i, d).wait_recv()
            hy[s, i, 1, beside[d], these] = hy[s, i, 1, beside[d], these] + ry1[s, i // 2, d]
            y2(s, i, d).start()

    def y_final(s, i):
        for d in range(2):
            y2(s, i, d).wait_recv()
        total = hy[s, i, 0, 0] + ry2[s, i, 0] + ry2[s, i, 1]
        if i % 2 == 1:
            yd(s, i).wait_recv()
            total = total + ryd[s, i // 2]
        hy[s, i, 0, 0] = total

    def y3(s, d):
        return put(hy.at[s, 0, 0, 0, pl.ds(2 * d, 2)], ry3.at[s, d], "y3", (s, d), at_x[way[d]])

    def y4(s, d):
        return put(hy.at[s, 1 + d, 0, 0], ry4.at[s, d], "y4", (s, d), at_x[way[d]])

    def y_on(s):
        for d in range(2):
            these = pl.ds(2 * d, 2)
            y3(s, d).wait_recv()
            hy[s, 1 + d, 0, 0, these] = hy[s, 1 + d, 0, 0, these] + ry3[s, d]
            y4(s, d).start()

    def zh(v, d):
        return put(hz.at[0, v, :, d, 2], rzh.at[v, d], "zh", (v, d), at_z[way[d]])

    def z3(v, d):
        return put(hz.at[0, v, :, :, 1 + 2 * d], rz3.at[v, d], "z3", (v, d), at_z[way[d]])

    def z2(v, d):
        return put(hz.at[d, v, :, :, 0], rz2.at[v, d], "z2", (v, d), at_z[2 * way[d]])

    def z1(v, d):
        return put(hz.at[1, v, :, :, 3 - 2 * d], rz1.at[v, d], "z1", (v, d), at_z[way[d]])

    def z_second(v):
        for d in range(2):
            zh(v, d).wait_recv()
            hz[0, v, :, d, 1 + 2 * d] = hz[0, v, :, d, 1 + 2 * d] + rzh[v, d]
            z3(v, d).start()

    def z_third(v, d):
        z3(v, d).wait_recv()
        hz[d, v, :, :, 0] = hz[d, v, :, :, 0] + rz3[v, d]
        z2(v, d).start()

    def z_final(v):
        for d in range(2):
            z2(v, d).wait_recv()
            z1(v, d).wait_recv()
        hz[1, v, :, :, 2] = (
            hz[1, v, :, :, 2] + (rz2[v, 0] + rz2[v, 1]) + (rz1[v, 0] + rz1[v, 1])
        )

    def z5(n):
        src = hz.at[1, 0, :, :, 2] if n == 0 else hz.at[1, 1:3, n - 1, :, 2]
        return put(src, rz5.at[n], "z5", n, at_x[(2, 1, -1)[n]])

    def z7(n):
        src = hz.at[1, 3, 1, beside[n], 2] if n < 2 else hz.at[1, 3, 0, 1, 2]
        return put(src, rz7.at[n], "z7", n, at_y[(1, -1, 2)[n]])

    def last(p, d):
        s, k = ((d - 2) % NZ) // 4, (d - 2) % 4
        src = hx.at[s, 3, 0, 0, k] if p == 0 else hy.at[s, 3, 0, 0, k]
        return put(src, rf.at[p, d - 1], "f", (p, d - 1), at_z[d])

    far, near = (2, 3, 4, 5), (6, 7, 1)

    def x_last():
        for d in range(2):
            x4(d).wait_recv()
        hx[0, 3, 0, 0] = hx[0, 3, 0, 0] + rx4[0] + rx4[1]
        for d in far:
            last(0, d).start()

    def y_last(s):
        for d in range(2):
            y4(s, d).wait_recv()
        hy[s, 3, 0, 0] = hy[s, 3, 0, 0] + ry4[s, 0] + ry4[s, 1]
        for d in (far, near)[s]:
            last(1, d).start()

    def events(u):
        s, v = lax.div(u, 4), lax.rem(u, 4)
        to_core(u).wait_recv()
        for p in range(2):
            i, h = piece(v, p)
            for g in range(2):
                rows = pl.ds(4 * g, 4)
                hx[s, i, h, g] = own[lax.rem(u, 2), p, rows, :TOP, :LANES] + got[u, p, rows, :TOP, :LANES]
                hy[s, i, h, g] = own[lax.rem(u, 2), p, rows, :TOP, LANES:] + got[u, p, rows, :TOP, LANES:]
                hz[s, v, p, g] = own[lax.rem(u, 2), p, rows, TOP:, :] + got[u, p, rows, TOP:, :]

        @pl.when(v == 0)
        def _():
            for d in range(2):
                x1(s, d).start()
            y_start(s, 0)

        @pl.when(v == 1)
        def _():
            x2(s, 0, 1).start()
            x2(s, 1, 0).start()
            y_start(s, 2)
            for d in range(2):
                y2(s, 1, d).start()

        @pl.when(v == 2)
        def _():
            yd(s, 1).start()

        @pl.when(v == 3)
        def _():
            yd(s, 3).start()
            for d in range(2):
                y2(s, 3, d).start()

        @pl.when(s == 0)
        def _():
            for d in range(2):
                zh(v, d).start()

        @pl.when(s == 1)
        def _():
            z_third(v, 1)
            for d in range(2):
                z1(v, d).start()

        @pl.when(u == 6)
        def _():
            x_on_way(1)
            y_next(1, 2)

    def late_events(u):
        s, v = lax.div(u, 4), lax.rem(u, 4)

        @pl.when(u == 2)
        def _():
            x_on_way(0)

        @pl.when((u >= 1) & (u < 5))
        def _():
            z_second(u - 1)

        @pl.when((u >= 3) & (u < 7))
        def _():
            z_third(u - 3, 0)

        @pl.when(v == 1)
        def _():
            y_next(s, 0)

        @pl.when(u == 2)
        def _():
            y_next(0, 2)

        @pl.when(u == 4)
        def _():
            x_final(0)
            for d in range(2):
                x3(d).start()
            y_final(0, 0)
            for d in range(2):
                y3(0, d).start()

        @pl.when(u == 5)
        def _():
            y_final(0, 1)
            y_final(0, 2)
            y_final(0, 3)

        @pl.when(u == 6)
        def _():
            x_on()
            y_on(0)
            z_final(0)
            z5(0).start()

        @pl.when(u == 7)
        def _():
            y_final(1, 0)
            for d in range(2):
                y3(1, d).start()

    def turn_units(u, _):
        @pl.when(u < UNITS)
        def _():
            product(1 - core, u, sent, u)

            @pl.when(u == 0)
            def _():
                pl.semaphore_wait(barrier, len(friends))

            to_core(u).start()

        @pl.when(u > 0)
        def _():
            events(u - 1)

        @pl.when(u < UNITS)
        def _():
            product(core, u, own, lax.rem(u, 2))

        @pl.when(u > 0)
        def _():
            late_events(u - 1)

        return 0

    def sent_units(u, _):
        to_core(u).wait_send()
        return 0

    def sent_quarters(v, _):
        for d in range(2):
            for sending in (zh, z3, z2, z1):
                sending(v, d).wait_send()
        return 0

    def sent_halves(s, _):
        yd(s, 1).wait_send()
        yd(s, 3).wait_send()
        for d in range(2):
            for sending in (x1, y3, y4):
                sending(s, d).wait_send()
            for h in range(2):
                x2(s, d, h).wait_send()
            for i in (0, 2):
                y1(s, i, d).wait_send()
            for i in range(4):
                y2(s, i, d).wait_send()
        return 0

    lax.fori_loop(0, UNITS + 1, turn_units, 0)

    x_final(1)
    for n, k in owners:
        x5(n, k).start()
    z_final(1)
    z_final(2)
    for n in (1, 2):
        z5(n).start()
    for load in small:
        load.wait()
    at_row = lax.broadcasted_iota(jnp.int32, (ROWS, LANES), 0)
    pair = jnp.zeros((ROWS, LANES), F32)
    for r in range(ROWS):
        pair = jnp.where(at_row == r, occ[blk // 2] + occ[(blk % 2) * ROWS + r], pair)
    for c in range(2):
        den[c] = (outer[x] + virt[pl.ds(2 * y_lo + c, 1), :]) - pair
    lax.fori_loop(0, UNITS, sent_units, 0)
    y_final(1, 1)
    y_final(1, 2)
    y_on(1)
    x_last()
    y_last(0)
    lax.fori_loop(0, 4, sent_quarters, 0)
    z_final(3)
    for n in range(3):
        z5(n).wait_recv()
    hz[1, 3, 0, :, 2] = hz[1, 3, 0, :, 2] + rz5[0, 0] + rz5[1, 1] + rz5[2, 0]
    hz[1, 3, 1, :, 2] = hz[1, 3, 1, :, 2] + rz5[0, 1] + rz5[1, 0] + rz5[2, 1]
    for n in range(3):
        z7(n).start()
    y_final(1, 3)
    y_last(1)
    lax.fori_loop(0, 2, sent_halves, 0)
    for d in range(2):
        x3(d).wait_send()
        x4(d).wait_send()
    for d in far:
        last(0, d).wait_send()

    total = hz[1, 3, 0, 0, 2]
    for n in range(3):
        z7(n).wait_recv()
        total = total + rz7[n]
    for p in range(2):
        lanes = slice(p * LANES, (p + 1) * LANES)
        out_ref[TOP:, lanes] = total[:, lanes] / den[p, TOP:]
    total = hx[1, 3, 0, 0, 2]
    for d in far:
        last(0, d).wait_recv()
        total = total + rf[0, d - 1]
    for n, k in owners:
        x5(n, k).wait_recv()
        total = total + rx5[n, k]
    out_ref[:TOP, :LANES] = total / den[0, :TOP]
    total = hy[1, 3, 0, 0, 2]
    for d in far + near:
        last(1, d).wait_recv()
        total = total + rf[1, d - 1]
    out_ref[:TOP, LANES:] = total / den[1, :TOP]

    for n in range(3):
        z5(n).wait_send()
        z7(n).wait_send()
    for n, k in owners:
        x5(n, k).wait_send()
    for d in far + near:
        last(1, d).wait_send()


def shards(amplitudes, integrals, occ_energy, virt_energy, outer_energy):
    depth = amplitudes.shape[0] * amplitudes.shape[1]
    t = amplitudes.reshape(depth, amplitudes.shape[2])
    w = integrals.reshape(depth, 4, 4, LANES).transpose(0, 2, 1, 3).reshape(depth * 16, LANES)
    virt = virt_energy.reshape(4, LANES)
    scratch = [pltpu.VMEM(shape, kind) for shape, kind in BUFFERS.values()]
    scratch += [pltpu.SMEM(occ_energy.shape, F32), pltpu.SMEM(outer_energy.shape, F32)]
    scratch += [pltpu.SemaphoreType.DMA((n,)) for n in (8, 8, 3)]
    for shape in SENDS.values():
        scratch += [pltpu.SemaphoreType.DMA(shape)] * 2
    return pl.pallas_call(
        kernel,
        out_shape=jax.ShapeDtypeStruct((ROWS, COLS), F32),
        in_specs=[pl.BlockSpec(memory_space=pl.ANY)] * 5,
        out_specs=pl.BlockSpec(memory_space=pltpu.VMEM),
        scratch_shapes=scratch,
        compiler_params=pltpu.CompilerParams(
            collective_id=0, has_side_effects=True, vmem_limit_bytes=56 * 2**20
        ),
    )(t, w, occ_energy, virt, outer_energy)


def solution(mesh):
    placed = (P("blk", "rep", None), P("blk", "rep", None, None), P(), P(), P())
    return jax.shard_map(
        shards, mesh=mesh, in_specs=placed, out_specs=P("blk", "rep"), check_vma=False
    )
```
